128 devices in a mesh: seq: 16 (over y_lo, z, core), samp: 8 (over y_hi, x).
Axes of the slice: x: 4, y: 4 (y_hi: 2, y_lo: 2; y = y_hi * 2 + y_lo), z: 4, core: 2. Of those that a mesh axis runs over, the one named last changes fastest.
Arguments:
- tokens: bfloat16 [32, 1024, 768], P('samp', 'seq'), may hold values from -6 to 6
- ada_scale: bfloat16 [32, 1024, 768], P('samp', 'seq'), may hold values from 0.19921875 to 1.796875
- ada_shift: bfloat16 [32, 1024, 768], P('samp', 'seq'), may hold values from -3 to 3
- out_gate: bfloat16 [32, 1024, 768], P('samp', 'seq'), may hold values from 0.049804688 to 0.94921875
- d_out: bfloat16 [32, 1024, 768], P('samp', 'seq'), may hold values from -6 to 6
- pair_bias: bfloat16 [16, 1024, 1024], P(None, 'seq', 'samp'), may hold values from -8 to 320
- key_mask: int32 [1024], replicated, may hold values 0 or 1
- w_query: bfloat16 [768, 768], replicated, may hold values from -0.21875 to 0.21875
- w_key: bfloat16 [768, 768], replicated, may hold values from -0.21875 to 0.21875
- w_value: bfloat16 [768, 768], replicated, may hold values from -0.21875 to 0.21875
- w_gate: bfloat16 [768, 768], replicated, may hold values from -0.21875 to 0.21875
- w_output: bfloat16 [768, 768], replicated, may hold values from -0.21875 to 0.21875
Outputs:
- d_tokens: bfloat16 [32, 1024, 768], P('samp', 'seq')
- d_ada_scale: bfloat16 [32, 1024, 768], P('samp', 'seq')
- d_ada_shift: bfloat16 [32, 1024, 768], P('samp', 'seq')
- d_out_gate: bfloat16 [32, 1024, 768], P('samp', 'seq')
- d_pair_bias: float32 [16, 1024, 1024], P(None, 'seq', 'samp')
- d_w_query: float32 [768, 768], replicated
- d_w_key: float32 [768, 768], replicated
- d_w_value: float32 [768, 768], replicated
- d_w_gate: float32 [768, 768], replicated
- d_w_output: float32 [768, 768], replicated
The draws below stay inside these ranges and needn't reach their ends.
All inputs are finite; a program needn't handle non-finite values.
Results may differ from the reference program's by a relative error of at most 0.023.
Values may be sent and summed in bfloat16 or wider, within the bound.
A program may use at most 192 MiB of HBM per device.

```python
import jax
import jax.numpy as jnp
from jax import lax

HEADS = 16
HEAD_SIZE = 48
D = 768
TOK_DEV = 64
SAMP_DEV = 4
TOKENS = 1024
SAMPLES = 32
N_SEQ = 16
N_SAMP = 8


def draw_pair_bias(key, part):
    key = jax.random.fold_in(key, 11)
    base_key = jax.random.fold_in(key, 0)
    bias_shape = (HEADS, TOKENS, TOKENS)
    values_drawn = jnp.clip(1.5 * jax.random.normal(base_key, bias_shape, jnp.float32), -8.0, 8.0)
    return values_drawn.astype(jnp.bfloat16)


def with_ends(drawn, stream_key, smallest, top_value):
    dims = drawn.shape
    place = [jax.random.randint(jax.random.fold_in(stream_key, axis), (), 0, dims[axis]) for axis in range(len(dims))]
    drawn = drawn.at[tuple(place)].set(smallest)
    longest = dims.index(max(dims))
    place[longest] = (place[longest] + 1) % dims[longest]
    return drawn.at[tuple(place)].set(top_value)


def steps_of(rng, shape, cuts, least, top_value):
    def one(axis_at, parts):
        steps = jax.random.uniform(jax.random.fold_in(jax.random.fold_in(rng, 6), axis_at), (parts,), jnp.float32, least / len(cuts), top_value / len(cuts))
        return jnp.repeat(jnp.exp(steps), shape[axis_at] // parts).reshape((-1,) + (1,) * (len(shape) - axis_at - 1))

    gain = one(*cuts[0])
    for cut in cuts[1:]:
        gain = gain * one(*cut)
    return gain


def bell_draw(rng, shape, spread, limit, shards=(), held_as=jnp.bfloat16):
    values = spread * jax.random.normal(rng, shape, jnp.float32)
    if shards:
        values = values * steps_of(rng, shape, shards, -0.22, 0.18)
    return jnp.clip(values, -limit, limit).astype(held_as)


def setup_inputs(seed: int = 0) -> dict:
    streams_of = jax.random.split(jax.random.key(seed), 13)
    tokens = bell_draw(streams_of[0], (SAMPLES, TOKENS, D), 1.0, 6.0, ((0, 8), (1, 16)))
    ada_scale = jnp.clip(0.19921875 + 1.5976562 * jax.random.uniform(streams_of[1], (SAMPLES, TOKENS, D), jnp.float32) ** steps_of(streams_of[1], (SAMPLES, TOKENS, D), ((0, 8), (1, 16)), -0.2, 0.2), 0.19921875, 1.796875).astype(jnp.bfloat16)
    ada_shift = bell_draw(streams_of[2], (SAMPLES, TOKENS, D), 0.5, 3.0, ((0, 8), (1, 16)))
    out_gate = jnp.clip(0.049804688 + 0.89941406 * jax.random.uniform(streams_of[3], (SAMPLES, TOKENS, D), jnp.float32) ** steps_of(streams_of[3], (SAMPLES, TOKENS, D), ((0, 8), (1, 16)), -0.2, 0.2), 0.049804688, 0.94921875).astype(jnp.bfloat16)
    d_out = bell_draw(streams_of[4], (SAMPLES, TOKENS, D), 1.0, 6.0, ((0, 8), (1, 16)))
    pair_bias = draw_pair_bias(jax.random.fold_in(streams_of[12], 71), 0)
    key_mask = with_ends((jax.random.randint(streams_of[6], (TOKENS,), 0, 8) < 7).astype(jnp.int32), jax.random.fold_in(streams_of[6], 1), 0, 1)
    w_query = bell_draw(streams_of[7], (D, D), D ** -0.5, 0.21875)
    w_key = bell_draw(streams_of[8], (D, D), D ** -0.5, 0.21875)
    w_value = bell_draw(streams_of[9], (D, D), D ** -0.5, 0.21875)
    w_gate = bell_draw(streams_of[10], (D, D), D ** -0.5, 0.21875)
    w_output = bell_draw(streams_of[11], (D, D), D ** -0.5, 0.21875)
    return {"tokens": tokens, "ada_scale": ada_scale, "ada_shift": ada_shift, "out_gate": out_gate, "d_out": d_out, "pair_bias": pair_bias, "key_mask": key_mask, "w_query": w_query, "w_key": w_key, "w_value": w_value, "w_gate": w_gate, "w_output": w_output}


norm_eps = 1e-05
masked_score = -1000000000.0

def sample_grads(token_row, scale_row, shift_row, gate_row, cotangent, pair_bias, key_mask, w_query, w_key, w_value, w_gate, w_output):
    score_scale = 1.0 / HEAD_SIZE ** 0.5
    token_values = token_row.astype(jnp.float32)
    row_mean = lax.optimization_barrier(jnp.mean(token_values, axis=-1, keepdims=True))
    centred = token_values - row_mean
    row_var = lax.optimization_barrier(jnp.mean(centred * centred, axis=-1, keepdims=True))
    inv_std = lax.rsqrt(row_var + norm_eps)
    normed = centred * inv_std
    adapted = (normed * scale_row.astype(jnp.float32) + shift_row.astype(jnp.float32)).astype(jnp.bfloat16)
    queries = jnp.dot(adapted, w_query, preferred_element_type=jnp.float32).astype(jnp.bfloat16)
    keys = jnp.dot(adapted, w_key, preferred_element_type=jnp.float32).astype(jnp.bfloat16)
    values = jnp.dot(adapted, w_value, preferred_element_type=jnp.float32).astype(jnp.bfloat16)
    gate_logits = jnp.dot(adapted, w_gate, preferred_element_type=jnp.float32)
    gate_sigmoid = jax.nn.sigmoid(gate_logits)
    query_heads = queries.astype(jnp.float32).reshape(TOKENS, HEADS, HEAD_SIZE)
    key_heads = keys.astype(jnp.float32).reshape(TOKENS, HEADS, HEAD_SIZE)
    value_heads = values.astype(jnp.float32).reshape(TOKENS, HEADS, HEAD_SIZE)
    live_keys = (key_mask > 0)[None, None, :]
    scores = jnp.einsum('ihd,jhd->hij', query_heads, key_heads) * score_scale + pair_bias.astype(jnp.float32)
    scores = jnp.where(live_keys, scores, masked_score)
    row_max = lax.optimization_barrier(jnp.max(scores, axis=-1, keepdims=True))
    expo = jnp.exp(scores - row_max)
    probs = expo / lax.optimization_barrier(jnp.sum(expo, axis=-1, keepdims=True))
    probs_b = probs.astype(jnp.bfloat16)
    attended = jnp.einsum('hij,jhd->ihd', probs_b.astype(jnp.float32), value_heads).reshape(TOKENS, D)
    gated = (gate_sigmoid * attended).astype(jnp.bfloat16)
    projected = jnp.dot(gated, w_output, preferred_element_type=jnp.float32)
    cotangent_values = cotangent.astype(jnp.float32)
    d_out_gate = (cotangent_values * projected).astype(jnp.bfloat16)
    d_projected = (cotangent_values * gate_row.astype(jnp.float32)).astype(jnp.bfloat16)
    grad_output = jnp.dot(gated.T, d_projected, preferred_element_type=jnp.float32)
    d_gated = jnp.dot(d_projected, w_output.T, preferred_element_type=jnp.float32)
    d_attended = (d_gated * gate_sigmoid).astype(jnp.bfloat16)
    d_gate_logits = (d_gated * attended * gate_sigmoid * (1.0 - gate_sigmoid)).astype(jnp.bfloat16)
    grad_gate = jnp.dot(adapted.T, d_gate_logits, preferred_element_type=jnp.float32)
    attended_heads = d_attended.astype(jnp.float32).reshape(TOKENS, HEADS, HEAD_SIZE)
    d_probs = jnp.einsum('ihd,jhd->hij', attended_heads, value_heads)
    delta = lax.optimization_barrier(jnp.sum(attended_heads * attended.reshape(TOKENS, HEADS, HEAD_SIZE), axis=-1))
    d_scores = jnp.where(live_keys, probs * (d_probs - delta.T[:, :, None]), 0.0).astype(jnp.bfloat16)
    score_grads = d_scores.astype(jnp.float32)
    d_queries = (jnp.einsum('hij,jhd->ihd', score_grads, key_heads) * score_scale).reshape(TOKENS, D).astype(jnp.bfloat16)
    score_blocks = score_grads.reshape(HEADS, N_SEQ, TOK_DEV, TOKENS)
    query_blocks = query_heads.reshape(N_SEQ, TOK_DEV, HEADS, HEAD_SIZE)
    key_parts = jnp.einsum('hbij,bihd->bjhd', score_blocks, query_blocks) * score_scale
    key_parts = lax.optimization_barrier(key_parts.astype(jnp.bfloat16))
    d_keys = lax.optimization_barrier(jnp.sum(key_parts.astype(jnp.float32), axis=0)).reshape(TOKENS, D).astype(jnp.bfloat16)
    prob_blocks = probs_b.astype(jnp.float32).reshape(HEADS, N_SEQ, TOK_DEV, TOKENS)
    grad_blocks = attended_heads.reshape(N_SEQ, TOK_DEV, HEADS, HEAD_SIZE)
    value_parts = jnp.einsum('hbij,bihd->bjhd', prob_blocks, grad_blocks)
    value_parts = lax.optimization_barrier(value_parts.astype(jnp.bfloat16))
    d_values = lax.optimization_barrier(jnp.sum(value_parts.astype(jnp.float32), axis=0)).reshape(TOKENS, D).astype(jnp.bfloat16)
    grad_query = jnp.dot(adapted.T, d_queries, preferred_element_type=jnp.float32)
    grad_key = jnp.dot(adapted.T, d_keys, preferred_element_type=jnp.float32)
    grad_value = jnp.dot(adapted.T, d_values, preferred_element_type=jnp.float32)
    d_adapted = jnp.dot(d_queries, w_query.T, preferred_element_type=jnp.float32)
    d_adapted = d_adapted + jnp.dot(d_keys, w_key.T, preferred_element_type=jnp.float32)
    d_adapted = d_adapted + jnp.dot(d_values, w_value.T, preferred_element_type=jnp.float32)
    d_adapted = d_adapted + jnp.dot(d_gate_logits, w_gate.T, preferred_element_type=jnp.float32)
    d_shift = d_adapted.astype(jnp.bfloat16)
    d_scale = (d_adapted * normed).astype(jnp.bfloat16)
    d_normed = d_adapted * scale_row.astype(jnp.float32)
    first_mean = lax.optimization_barrier(jnp.mean(d_normed, axis=-1, keepdims=True))
    second_mean = lax.optimization_barrier(jnp.mean(d_normed * normed, axis=-1, keepdims=True))
    d_tokens = (cotangent_values + inv_std * (d_normed - first_mean - normed * second_mean)).astype(jnp.bfloat16)
    return ((d_tokens, d_scale, d_shift, d_out_gate), score_grads, (grad_query, grad_key, grad_value, grad_gate, grad_output))

def reference(tokens, ada_scale, ada_shift, out_gate, d_out, pair_bias, key_mask, w_query, w_key, w_value, w_gate, w_output):

    def one_sample(running, per_sample):
        run_bias, weight_sums = running
        rows, score_grads, weight_grads = sample_grads(per_sample[0], per_sample[1], per_sample[2], per_sample[3], per_sample[4], pair_bias, key_mask, w_query, w_key, w_value, w_gate, w_output)
        weight_sums = tuple((total + term for total, term in zip(weight_sums, weight_grads)))
        return ((run_bias + score_grads, weight_sums), rows)

    def one_run(running, per_run):
        bias_total, weight_sums = running
        start_run = (jnp.zeros((HEADS, TOKENS, TOKENS), jnp.float32), weight_sums)
        final_run, run_rows = lax.scan(one_sample, start_run, per_run)
        run_bias, weight_sums = final_run
        rounded = lax.optimization_barrier(run_bias.astype(jnp.bfloat16))
        return ((bias_total + rounded.astype(jnp.float32), weight_sums), run_rows)

    def runs_of(array):
        return array.reshape(N_SAMP, SAMP_DEV, TOKENS, D)
    zero_weight = jnp.zeros((D, D), jnp.float32)
    start = (jnp.zeros((HEADS, TOKENS, TOKENS), jnp.float32), (zero_weight, zero_weight, zero_weight, zero_weight, zero_weight))
    grouped = (runs_of(tokens), runs_of(ada_scale), runs_of(ada_shift), runs_of(out_gate), runs_of(d_out))
    final, stacked = lax.scan(one_run, start, grouped)
    bias_sum, weight_sums = final
    flat = tuple((piece.reshape(SAMPLES, TOKENS, D) for piece in stacked))
    return (flat[0], flat[1], flat[2], flat[3], bias_sum, weight_sums[0], weight_sums[1], weight_sums[2], weight_sums[3], weight_sums[4])
```

```python
import functools
import math

import jax
import jax.numpy as jnp
from jax import lax
from jax.experimental import pallas as pl
from jax.experimental.pallas import tpu as pltpu
from jax.sharding import PartitionSpec as P

norm_eps = 1e-05
masked_score = -1e9
HS = 48
LOG2E = 1.4426950408889634
LN2 = 0.6931471805599453
f32 = jnp.float32
bf16 = jnp.bfloat16
V = pltpu.VMEM
VMEM_LIMIT = 56 << 20


def spec():
    return pl.BlockSpec(memory_space=V)


def dot(a, b, ca=1, cb=0):
    return lax.dot_general(a, b, (((ca,), (cb,)), ((), ())), preferred_element_type=f32)


def norm_rows(x):
    mean = jnp.mean(x, axis=-1, keepdims=True)
    centred = x - mean
    var = jnp.mean(centred * centred, axis=-1, keepdims=True)
    inv = lax.rsqrt(var + norm_eps)
    return centred * inv, inv


def rows_kernel(tok, scale, shift, og, dout, wq, wk, wv, wg, wo, send, adT, sig, dgated, dproj):
    normed, _ = norm_rows(tok[...].astype(f32))
    adapted = (normed * scale[...].astype(f32) + shift[...].astype(f32)).astype(bf16)
    adT[...] = jnp.transpose(adapted)
    gs = jax.nn.sigmoid(dot(adapted, wg[...]))
    sig[...] = gs
    dp = (dout[...].astype(f32) * og[...].astype(f32)).astype(bf16)
    dproj[...] = dp
    dg = dot(dp, wo[...], 1, 1)
    dgated[...] = dg

    def put(t, val):
        vt = jnp.transpose(val.astype(bf16))
        for h in range(16):
            send[h, HS * t : HS * t + HS, :] = vt[HS * h : HS * h + HS, :]

    put(0, dot(adapted, wq[...]) * (LOG2E / math.sqrt(HS)))
    put(1, dot(adapted, wk[...]))
    put(2, dot(adapted, wv[...]))
    put(3, dg * gs)


def attn_kernel(recv_ref, mask_ref, bias_ref, send_ref, dbias_ref, bm, acc, xs, qn, an, kn, vn, dkv, R=256):
    T = 1024
    live = mask_ref[...] > 0
    livef = live.astype(f32)

    def prep(i, c):
        rows = pl.ds(pl.multiple_of(i * 128, 128), 128)
        for b in range(8):
            sl = slice(128 * b, 128 * b + 128)
            bm[rows, sl] = jnp.where(live[:, sl], bias_ref[b, rows, :].astype(f32) * LOG2E, masked_score)
        return c

    lax.fori_loop(0, T // 128, prep, 0)

    for s in range(4):
        p, half = s // 2, s % 2
        lanes = slice(128 * p + 64 * half, 128 * p + 64 * half + 64)
        for b in range(8):
            xs[s, :, 128 * b : 128 * b + 128] = jnp.concatenate(
                [recv_ref[2 * b, :, lanes], recv_ref[2 * b + 1, :, lanes]], axis=1
            )

    def sample(s, c):
        kTm = jnp.where(live, xs[s, 48:96, :].astype(f32), 0.0).astype(bf16)
        vT = xs[s, 96:144, :]
        qn[...] = jnp.transpose(xs[s, 0:48, :])
        an[...] = jnp.transpose(xs[s, 144:192, :])
        kn[...] = jnp.transpose(kTm)
        vn[...] = jnp.transpose(vT)
        vext = jnp.concatenate([vT, jnp.ones((16, T), bf16)], axis=0)
        dkv[...] = jnp.zeros_like(dkv)

        def block(i, c2):
            rows = pl.ds(pl.multiple_of(i * R, R), R)
            S = dot(qn[rows, :], kTm) + bm[rows, :]
            m = jnp.max(S, axis=1, keepdims=True)
            e = jnp.exp2(S - m)
            rinv = 1.0 / jnp.sum(e, axis=1, keepdims=True)
            eb = e.astype(bf16)
            att = dot(eb, vn[...]) * rinv
            da = (an[rows, :].astype(f32) * rinv).astype(bf16)
            delta = jnp.sum(da.astype(f32) * att, axis=1, keepdims=True)
            hi = delta.astype(bf16)
            lo = (delta - hi.astype(f32)).astype(bf16)
            daext = jnp.concatenate([da, -hi, -lo, jnp.zeros((R, 14), bf16)], axis=1)
            dS = e * dot(daext, vext)
            dSb = dS.astype(bf16)

            @pl.when(s == 0)
            def _():
                acc[rows, :] = dS

            @pl.when(s > 0)
            def _():
                acc[rows, :] += dS

            dq = dot(dSb, kn[...]) * (1.0 / math.sqrt(HS))
            dkv[0:48, :] += dot(xs[s, 0:48, rows], dSb)
            dkv[48:96, :] += dot(jnp.transpose(da), eb)
            xs[s, 0:96, rows] = jnp.transpose(jnp.concatenate([att, dq], axis=1).astype(bf16))
            return c2

        lax.fori_loop(0, T // R, block, 0)
        xs[s, 96:144, :] = (dkv[0:48, :] * (livef * LN2)).astype(bf16)
        xs[s, 144:192, :] = dkv[48:96, :].astype(bf16)
        return c

    lax.fori_loop(0, 4, sample, 0)

    for b in range(8):
        for half in range(2):
            lanes = slice(128 * b + 64 * half, 128 * b + 64 * half + 64)
            for p in range(2):
                send_ref[2 * b + half, :, 128 * p : 128 * p + 128] = jnp.concatenate(
                    [xs[2 * p, :, lanes], xs[2 * p + 1, :, lanes]], axis=1
                )

    def fin(i, c):
        rows = pl.ds(pl.multiple_of(i * 128, 128), 128)
        for b in range(8):
            sl = slice(128 * b, 128 * b + 128)
            dbias_ref[b, rows, :] = (acc[rows, sl] * livef[:, sl]).astype(bf16)
        return c

    lax.fori_loop(0, T // 128, fin, 0)


def grads_kernel(recv, tok, scale, dout, adT, sig, dgated, dproj, wq, wk, wv, wg, wo,
                 dtok, dscale, dshift, dog, G):
    def get(t):
        xT = jnp.concatenate([recv[h, HS * t : HS * t + HS, :] for h in range(16)], axis=0)
        return jnp.transpose(xT)

    def put(m, val):
        for j in range(6):
            G[j, 768 * m : 768 * m + 768, :] = val[:, 128 * j : 128 * j + 128].astype(bf16)

    cot = dout[...].astype(f32)
    gs = sig[...]
    att = get(0).astype(f32)
    gated = (gs * att).astype(bf16)
    dog[...] = (cot * dot(gated, wo[...])).astype(bf16)
    put(4, dot(gated, dproj[...], 0, 0))
    dgl = (dgated[...] * att * gs * (1.0 - gs)).astype(bf16)
    put(3, dot(adT[...], dgl))
    d_ad = dot(dgl, wg[...], 1, 1)
    for m, w in ((0, wq), (1, wk), (2, wv)):
        dx = get(m + 1)
        put(m, dot(adT[...], dx))
        d_ad = d_ad + dot(dx, w[...], 1, 1)
    normed, inv = norm_rows(tok[...].astype(f32))
    dshift[...] = d_ad.astype(bf16)
    dscale[...] = (d_ad * normed).astype(bf16)
    dn = d_ad * scale[...].astype(f32)
    m1 = jnp.mean(dn, axis=-1, keepdims=True)
    m2 = jnp.mean(dn * normed, axis=-1, keepdims=True)
    dtok[...] = (cot + inv * (dn - m1 - normed * m2)).astype(bf16)


def sds(shape, dtype):
    return jax.ShapeDtypeStruct(shape, dtype)


def on_device(tokens, ada_scale, ada_shift, out_gate, d_out, pair_bias, key_mask,
              w_query, w_key, w_value, w_gate, w_output):
    params = pltpu.CompilerParams(vmem_limit_bytes=VMEM_LIMIT)
    rows = lambda a: a.reshape(256, 768)
    tok, scale, shift, og, cot = map(rows, (tokens, ada_scale, ada_shift, out_gate, d_out))
    bias_mine = lax.all_to_all(pair_bias, "seq", split_axis=0, concat_axis=1, tiled=True)
    bias_full = lax.all_gather(bias_mine.reshape(1024, 128), "samp", axis=0)
    send, adT, sig, dgated, dproj = pl.pallas_call(
        rows_kernel,
        out_shape=(sds((16, 192, 256), bf16), sds((768, 256), bf16), sds((256, 768), f32),
                   sds((256, 768), f32), sds((256, 768), bf16)),
        in_specs=[spec()] * 10,
        out_specs=[spec()] * 5,
        compiler_params=params,
        cost_estimate=pl.CostEstimate(flops=5 * 2 * 256 * 768 * 768, bytes_accessed=10 << 20, transcendentals=256 * 768),
    )(tok, scale, shift, og, cot, w_query, w_key, w_value, w_gate, w_output)
    recv = lax.all_to_all(send, "seq", split_axis=0, concat_axis=0, tiled=True)
    back, dbias = pl.pallas_call(
        attn_kernel,
        out_shape=(sds((16, 192, 256), bf16), sds((8, 1024, 128), bf16)),
        in_specs=[spec()] * 3,
        out_specs=[spec()] * 2,
        scratch_shapes=[V((1024, 1024), f32), V((1024, 1024), f32), V((4, 192, 1024), bf16),
                        V((1024, 48), bf16), V((1024, 48), bf16), V((1024, 48), bf16), V((1024, 48), bf16),
                        V((96, 1024), f32)],
        compiler_params=params,
        cost_estimate=pl.CostEstimate(flops=12 * 4 * 1024 * 1024 * 48, bytes_accessed=10 << 20, transcendentals=4 << 20),
    )(recv, key_mask.reshape(1, 1024), bias_full)
    back = lax.all_to_all(back, "seq", split_axis=0, concat_axis=0, tiled=True)
    bias_sum = lax.psum_scatter(dbias, "samp", scatter_dimension=0, tiled=True)
    dtok, dscale, dshift, dog, G = pl.pallas_call(
        grads_kernel,
        out_shape=(sds((256, 768), bf16),) * 4 + (sds((6, 3840, 128), bf16),),
        in_specs=[spec()] * 13,
        out_specs=[spec()] * 5,
        compiler_params=params,
        cost_estimate=pl.CostEstimate(flops=10 * 2 * 256 * 768 * 768, bytes_accessed=20 << 20, transcendentals=0),
    )(back, tok, scale, cot, adT, sig, dgated, dproj, w_query, w_key, w_value, w_gate, w_output)
    d_pair = lax.all_to_all(bias_sum.reshape(16, 64, 128), "seq", split_axis=0, concat_axis=0, tiled=True).astype(f32)
    G = lax.psum(G, ("seq", "samp"))
    grads = G.reshape(6, 5, 768, 128).transpose(1, 2, 0, 3).reshape(5, 768, 768).astype(f32)
    shaped = lambda a: a.reshape(4, 64, 768)
    return (shaped(dtok), shaped(dscale), shaped(dshift), shaped(dog), d_pair,
            grads[0], grads[1], grads[2], grads[3], grads[4])


def solution(mesh):
    act = P("samp", "seq", None)
    tile = P(None, "seq", "samp")
    return jax.shard_map(
        on_device,
        mesh=mesh,
        in_specs=(act,) * 5 + (tile,) + (P(),) * 6,
        out_specs=(act,) * 4 + (tile,) + (P(),) * 5,
        check_vma=False,
    )
```

```python
import functools
import math

import jax
import jax.numpy as jnp
from jax import lax
from jax.experimental import pallas as pl
from jax.experimental.pallas import tpu as pltpu
from jax.sharding import PartitionSpec as P

norm_eps = 1e-05
masked_score = -1e9
HS = 48
LOG2E = 1.4426950408889634
LN2 = 0.6931471805599453
f32 = jnp.float32
bf16 = jnp.bfloat16
V = pltpu.VMEM
VMEM_LIMIT = 56 << 20


def spec():
    return pl.BlockSpec(memory_space=V)


def dot(a, b, ca=1, cb=0):
    return lax.dot_general(a, b, (((ca,), (cb,)), ((), ())), preferred_element_type=f32)


def norm_rows(x):
    mean = jnp.mean(x, axis=-1, keepdims=True)
    centred = x - mean
    var = jnp.mean(centred * centred, axis=-1, keepdims=True)
    inv = lax.rsqrt(var + norm_eps)
    return centred * inv, inv


def rows_kernel(tok, scale, shift, og, dout, wq, wk, wv, wg, wo, send, adT, sig, dgated, dproj):
    normed, _ = norm_rows(tok[...].astype(f32))
    adapted = (normed * scale[...].astype(f32) + shift[...].astype(f32)).astype(bf16)
    adT[...] = jnp.transpose(adapted)
    gs = jax.nn.sigmoid(dot(adapted, wg[...]))
    sig[...] = gs
    dp = (dout[...].astype(f32) * og[...].astype(f32)).astype(bf16)
    dproj[...] = dp
    dg = dot(dp, wo[...], 1, 1)
    dgated[...] = dg

    def put(t, val):
        vt = jnp.transpose(val.astype(bf16))
        for h in range(16):
            send[h, HS * t : HS * t + HS, :] = vt[HS * h : HS * h + HS, :]

    put(0, dot(adapted, wq[...]) * (LOG2E / math.sqrt(HS)))
    put(1, dot(adapted, wk[...]))
    put(2, dot(adapted, wv[...]))
    put(3, dg * gs)


def attn_kernel(recv_ref, mask_ref, bias_ref, send_ref, dbias_ref, bm, acc, xs, qn, an, kn, vn, dkv, R=256):
    T = 1024
    live = mask_ref[...] > 0
    livef = live.astype(f32)

    def prep(i, c):
        rows = pl.ds(pl.multiple_of(i * 128, 128), 128)
        for b in range(8):
            sl = slice(128 * b, 128 * b + 128)
            bm[rows, sl] = jnp.where(live[:, sl], bias_ref[b, rows, :].astype(f32) * LOG2E, masked_score)
        return c

    lax.fori_loop(0, T // 128, prep, 0)

    for s in range(4):
        p, half = s // 2, s % 2
        lanes = slice(128 * p + 64 * half, 128 * p + 64 * half + 64)
        for b in range(8):
            xs[s, :, 128 * b : 128 * b + 128] = jnp.concatenate(
                [recv_ref[2 * b, :, lanes], recv_ref[2 * b + 1, :, lanes]], axis=1
            )

    def sample(s, c):
        kTm = jnp.where(live, xs[s, 48:96, :].astype(f32), 0.0).astype(bf16)
        vT = xs[s, 96:144, :]
        qn[...] = jnp.transpose(xs[s, 0:48, :])
        an[...] = jnp.transpose(xs[s, 144:192, :])
        kn[...] = jnp.transpose(kTm)
        vn[...] = jnp.transpose(vT)
        vext = jnp.concatenate([vT, jnp.ones((16, T), bf16)], axis=0)
        dkv[...] = jnp.zeros_like(dkv)

        def block(i, c2):
            rows = pl.ds(pl.multiple_of(i * R, R), R)
            S = dot(qn[rows, :], kTm) + bm[rows, :]
            m = jnp.max(S, axis=1, keepdims=True)
            e = jnp.exp2(S - m)
            rinv = 1.0 / jnp.sum(e, axis=1, keepdims=True)
            eb = e.astype(bf16)
            att = dot(eb, vn[...]) * rinv
            da = (an[rows, :].astype(f32) * rinv).astype(bf16)
            delta = jnp.sum(da.astype(f32) * att, axis=1, keepdims=True)
            hi = delta.astype(bf16)
            lo = (delta - hi.astype(f32)).astype(bf16)
            daext = jnp.concatenate([da, -hi, -lo, jnp.zeros((R, 14), bf16)], axis=1)
            dS = e * dot(daext, vext)
            dSb = dS.astype(bf16)

            @pl.when(s == 0)
            def _():
                acc[rows, :] = dS

            @pl.when(s > 0)
            def _():
                acc[rows, :] += dS

            dq = dot(dSb, kn[...]) * (1.0 / math.sqrt(HS))
            dkv[0:48, :] += dot(xs[s, 0:48, rows], dSb)
            dkv[48:96, :] += dot(jnp.transpose(da), eb)
            xs[s, 0:96, rows] = jnp.transpose(jnp.concatenate([att, dq], axis=1).astype(bf16))
            return c2

        lax.fori_loop(0, T // R, block, 0)
        xs[s, 96:144, :] = (dkv[0:48, :] * (livef * LN2)).astype(bf16)
        xs[s, 144:192, :] = dkv[48:96, :].astype(bf16)
        return c

    lax.fori_loop(0, 4, sample, 0)

    for b in range(8):
        for half in range(2):
            lanes = slice(128 * b + 64 * half, 128 * b + 64 * half + 64)
            for p in range(2):
                send_ref[2 * b + half, :, 128 * p : 128 * p + 128] = jnp.concatenate(
                    [xs[2 * p, :, lanes], xs[2 * p + 1, :, lanes]], axis=1
                )

    def fin(i, c):
        rows = pl.ds(pl.multiple_of(i * 128, 128), 128)
        for b in range(8):
            sl = slice(128 * b, 128 * b + 128)
            dbias_ref[b, rows, :] = (acc[rows, sl] * livef[:, sl]).astype(bf16)
        return c

    lax.fori_loop(0, T // 128, fin, 0)


def position():
    seq, samp = lax.axis_index("seq"), lax.axis_index("samp")
    return {
        "seq": seq,
        "samp": samp,
        "core": lax.rem(seq, 2),
        "z": lax.rem(seq // 2, 4),
        "x": lax.rem(samp, 4),
        "y": (samp // 4) * 2 + seq // 8,
    }


def along(pos, axis, step):
    new = dict(pos)
    new[axis] = lax.rem(pos[axis] + step, 4)
    return ((lax.rem(new["y"], 2)) * 8 + new["z"] * 2 + pos["core"], (new["y"] // 2) * 4 + new["x"])


def seq_peer(pos, step):
    return (lax.rem(pos["seq"] + step, 16), pos["samp"])


def samp_peer(pos, step):
    return (pos["seq"], lax.rem(pos["samp"] + step, 8))


def core_peer(pos):
    return (pos["seq"] + 1 - 2 * pos["core"], pos["samp"])


def remote(src, dst, ss, rs, dev):
    return pltpu.make_async_remote_copy(
        src_ref=src, dst_ref=dst, send_sem=ss, recv_sem=rs, device_id=dev, device_id_type=pl.DeviceIdType.MESH
    )


def greet(devices):
    barrier = pltpu.get_barrier_semaphore()
    for d in devices:
        pl.semaphore_signal(barrier, inc=1, device_id=d, device_id_type=pl.DeviceIdType.MESH)
    return lambda: pl.semaphore_wait(barrier, len(devices))


AXES = (("x", "y", "z"), ("y", "z", "x"), ("z", "x", "y"))


def grads_kernel(recv, dbias, tok, scale, dout, adT, sig, dgated, dproj, wq, wk, wv, wg, wo,
                 dtok, dscale, dshift, dog, F, dpair,
                 G, R0, R1, B1, R2, R3, DB, SB, RP,
                 s0s, s0r, s1s, s1r, s2s, s2r, s3s, s3r, g2s, g2r, g1s, g1r, gcs, gcr, dbs, dbr, prs, prr):
    pos = position()
    core = pos["core"]
    other = 1 - core
    mine = [core * 3 + p for p in range(3)]
    peers = [seq_peer(pos, k) for k in range(1, 16)] + [samp_peer(pos, k) for k in range(1, 8)]
    far_y = along(pos, "y", jnp.where(lax.rem(pos["y"], 2) == 0, 3, 1))
    arrived = greet(peers + [far_y])

    normed, inv = norm_rows(tok[...].astype(f32))
    arrived()

    db_copies = []
    for k in range(1, 8):
        dev = samp_peer(pos, k)
        c = remote(dbias.at[dev[1]], DB.at[k - 1], dbs.at[k - 1], dbr.at[k - 1], dev)
        c.start()
        db_copies.append(c)

    def get(t):
        xT = jnp.concatenate([recv[h, HS * t : HS * t + HS, :] for h in range(16)], axis=0)
        return jnp.transpose(xT)

    first = []

    def put(m, val):
        rows = slice(768 * m, 768 * m + 768)
        for j in range(6):
            G[j, rows, :] = val[:, 128 * j : 128 * j + 128].astype(bf16)
        for p in range(3):
            c = remote(G.at[other * 3 + p, rows], R0.at[p, rows], s0s.at[p, m], s0r.at[p, m], core_peer(pos))
            c.start()
            first.append(c)

    cot = dout[...].astype(f32)
    gs = sig[...]
    att = get(0).astype(f32)
    gated = (gs * att).astype(bf16)
    put(4, dot(gated, dproj[...], 0, 0))
    dgl = (dgated[...] * att * gs * (1.0 - gs)).astype(bf16)
    put(3, dot(adT[...], dgl))
    dxs = []
    for m in range(3):
        dxs.append(get(m + 1))
        put(m, dot(adT[...], dxs[m]))

    for c in first:
        c.wait()

    def add0(p):
        def body(i, carry):
            rows = pl.ds(pl.multiple_of(i * 960, 960), 960)
            j = mine[p]
            G[j, rows, :] = (G[j, rows, :].astype(f32) + R0[p, rows, :].astype(f32)).astype(bf16)
            return carry
        lax.fori_loop(0, 4, body, 0)

    def quarter(i):
        return pl.ds(pl.multiple_of(i * 960, 960), 960)

    def piece(i):
        return pl.ds(pl.multiple_of(i * 240, 240), 240)

    c1 = []
    for p in range(3):
        add0(p)
        a1 = AXES[p][0]
        for k in range(1, 4):
            t = lax.rem(pos[a1] + k, 4)
            c = remote(G.at[mine[p], quarter(t)], R1.at[p, k - 1], s1s.at[p, k - 1], s1r.at[p, k - 1], along(pos, a1, k))
            c.start()
            c1.append(c)

    dog[...] = (cot * dot(gated, wo[...])).astype(bf16)
    d_ad = dot(dgl, wg[...], 1, 1)
    for m, w in enumerate((wq, wk, wv)):
        d_ad = d_ad + dot(dxs[m], w[...], 1, 1)
    dshift[...] = d_ad.astype(bf16)
    dscale[...] = (d_ad * normed).astype(bf16)
    dn = d_ad * scale[...].astype(f32)
    m1 = jnp.mean(dn, axis=-1, keepdims=True)
    m2 = jnp.mean(dn * normed, axis=-1, keepdims=True)
    dtok[...] = (cot + inv * (dn - m1 - normed * m2)).astype(bf16)

    c2 = []
    for p in range(3):
        for c in c1[3 * p : 3 * p + 3]:
            c.wait()
        a1, a2 = AXES[p][0], AXES[p][1]
        own = quarter(pos[a1])
        B1[p] = (G[mine[p], own, :].astype(f32) + R1[p, 0].astype(f32) + R1[p, 1].astype(f32) + R1[p, 2].astype(f32)).astype(bf16)
        for k in range(1, 4):
            t = lax.rem(pos[a2] + k, 4)
            c = remote(B1.at[p, piece(t)], R2.at[p, k - 1], s2s.at[p, k - 1], s2r.at[p, k - 1], along(pos, a2, k))
            c.start()
            c2.append(c)

    c3 = []
    for p in range(3):
        for c in c2[3 * p : 3 * p + 3]:
            c.wait()
        a2, a3 = AXES[p][1], AXES[p][2]
        at = pos[a3]
        R3[p, at] = (B1[p, piece(pos[a2]), :].astype(f32) + R2[p, 0].astype(f32) + R2[p, 1].astype(f32) + R2[p, 2].astype(f32)).astype(bf16)
        for k in range(1, 4):
            c = remote(R3.at[p, at], R3.at[p, at], s3s.at[p, k - 1], s3r.at[p, k - 1], along(pos, a3, k))
            c.start()
            c3.append(c)

    cg2 = []
    for p in range(3):
        for c in c3[3 * p : 3 * p + 3]:
            c.wait()
        a1, a2 = AXES[p][0], AXES[p][1]
        rows = pl.ds(pl.multiple_of(pos[a1] * 960 + pos[a2] * 240, 240), 240)
        F[mine[p], rows, :] = (R3[p, 0].astype(f32) + R3[p, 1].astype(f32) + R3[p, 2].astype(f32) + R3[p, 3].astype(f32)).astype(bf16)
        for k in range(1, 4):
            c = remote(F.at[mine[p], rows], F.at[mine[p], rows], g2s.at[p, k - 1], g2r.at[p, k - 1], along(pos, a2, k))
            c.start()
            cg2.append(c)

    cg1 = []
    cgc = []

    def to_core(p, k, t):
        c = remote(F.at[mine[p], quarter(t)], F.at[mine[p], quarter(t)], gcs.at[p, k], gcr.at[p, k], core_peer(pos))
        c.start()
        cgc.append(c)

    for p in range(3):
        for c in cg2[3 * p : 3 * p + 3]:
            c.wait()
        a1 = AXES[p][0]
        own = quarter(pos[a1])
        for k in range(1, 4):
            c = remote(F.at[mine[p], own], F.at[mine[p], own], g1s.at[p, k - 1], g1r.at[p, k - 1], along(pos, a1, k))
            c.start()
            cg1.append(c)
        to_core(p, 0, pos[a1])

    for c in db_copies:
        c.wait()
    def sum_bias(i, carry):
        rows = pl.ds(pl.multiple_of(i * 128, 128), 128)
        tot = dbias[pos["samp"], rows, :].astype(f32)
        for k in range(7):
            tot = tot + DB[k, rows, :].astype(f32)
        SB[rows, :] = tot.astype(bf16)
        return carry
    lax.fori_loop(0, 8, sum_bias, 0)
    pr = []
    for k in range(1, 16):
        dev = seq_peer(pos, k)
        rows = pl.ds(pl.multiple_of(dev[0] * 64, 64), 64)
        c = remote(SB.at[rows], RP.at[pos["seq"]], prs.at[k - 1], prr.at[k - 1], dev)
        c.start()
        pr.append(c)
    RP[pos["seq"]] = SB[pl.ds(pl.multiple_of(pos["seq"] * 64, 64), 64), :]

    for p in range(3):
        for k in range(1, 4):
            cg1[3 * p + k - 1].wait()
            to_core(p, k, lax.rem(pos[AXES[p][0]] + 4 - k, 4))
    for c in pr:
        c.wait()
    dpair[...] = RP[...].astype(f32)
    for c in cgc:
        c.wait()


def widen_kernel(F, *outs):
    for m in range(5):
        for j in range(6):
            outs[m][:, 128 * j : 128 * j + 128] = F[j, m].astype(f32)


def sds(shape, dtype):
    return jax.ShapeDtypeStruct(shape, dtype)


def on_device(tokens, ada_scale, ada_shift, out_gate, d_out, pair_bias, key_mask,
              w_query, w_key, w_value, w_gate, w_output):
    params = pltpu.CompilerParams(vmem_limit_bytes=VMEM_LIMIT)
    rows = lambda a: a.reshape(256, 768)
    tok, scale, shift, og, cot = map(rows, (tokens, ada_scale, ada_shift, out_gate, d_out))
    bias_mine = lax.all_to_all(pair_bias, "seq", split_axis=0, concat_axis=1, tiled=True)
    bias_full = lax.all_gather(bias_mine.reshape(1024, 128), "samp", axis=0)
    send, adT, sig, dgated, dproj = pl.pallas_call(
        rows_kernel,
        out_shape=(sds((16, 192, 256), bf16), sds((768, 256), bf16), sds((256, 768), f32),
                   sds((256, 768), f32), sds((256, 768), bf16)),
        in_specs=[spec()] * 10,
        out_specs=[spec()] * 5,
        compiler_params=params,
        cost_estimate=pl.CostEstimate(flops=5 * 2 * 256 * 768 * 768, bytes_accessed=10 << 20, transcendentals=256 * 768),
    )(tok, scale, shift, og, cot, w_query, w_key, w_value, w_gate, w_output)
    recv = lax.all_to_all(send, "seq", split_axis=0, concat_axis=0, tiled=True)
    back, dbias = pl.pallas_call(
        attn_kernel,
        out_shape=(sds((16, 192, 256), bf16), sds((8, 1024, 128), bf16)),
        in_specs=[spec()] * 3,
        out_specs=[spec()] * 2,
        scratch_shapes=[V((1024, 1024), f32), V((1024, 1024), f32), V((4, 192, 1024), bf16),
                        V((1024, 48), bf16), V((1024, 48), bf16), V((1024, 48), bf16), V((1024, 48), bf16),
                        V((96, 1024), f32)],
        compiler_params=params,
        cost_estimate=pl.CostEstimate(flops=12 * 4 * 1024 * 1024 * 48, bytes_accessed=10 << 20, transcendentals=4 << 20),
    )(recv, key_mask.reshape(1, 1024), bias_full)
    back = lax.all_to_all(back, "seq", split_axis=0, concat_axis=0, tiled=True)
    dma = lambda *shape: pltpu.SemaphoreType.DMA(shape)
    dtok, dscale, dshift, dog, F, d_pair = pl.pallas_call(
        grads_kernel,
        out_shape=(sds((256, 768), bf16),) * 4 + (sds((6, 3840, 128), bf16), sds((16, 64, 128), f32)),
        in_specs=[spec()] * 14,
        out_specs=[spec()] * 6,
        scratch_shapes=[V((6, 3840, 128), bf16), V((3, 3840, 128), bf16), V((3, 3, 960, 128), bf16), V((3, 960, 128), bf16),
                        V((3, 3, 240, 128), bf16), V((3, 4, 240, 128), bf16), V((7, 1024, 128), bf16), V((1024, 128), bf16),
                        V((16, 64, 128), bf16)]
        + [dma(3, 5)] * 2 + [dma(3, 3)] * 10 + [dma(3, 4)] * 2 + [dma(7)] * 2 + [dma(15)] * 2,
        compiler_params=pltpu.CompilerParams(vmem_limit_bytes=VMEM_LIMIT, collective_id=2, has_side_effects=True),
        cost_estimate=pl.CostEstimate(flops=10 * 2 * 256 * 768 * 768, bytes_accessed=20 << 20, transcendentals=0),
    )(back, dbias, tok, scale, cot, adT, sig, dgated, dproj, w_query, w_key, w_value, w_gate, w_output)
    grads = pl.pallas_call(
        widen_kernel,
        grid=(6,),
        out_shape=(sds((768, 768), f32),) * 5,
        in_specs=[pl.BlockSpec((6, 5, 128, 128), lambda i: (0, 0, i, 0))],
        out_specs=[pl.BlockSpec((128, 768), lambda i: (i, 0))] * 5,
    )(F.reshape(6, 5, 768, 128))
    shaped = lambda a: a.reshape(4, 64, 768)
    return (shaped(dtok), shaped(dscale), shaped(dshift), shaped(dog), d_pair,
            grads[0], grads[1], grads[2], grads[3], grads[4])


def solution(mesh):
    act = P("samp", "seq", None)
    tile = P(None, "seq", "samp")
    return jax.shard_map(
        on_device,
        mesh=mesh,
        in_specs=(act,) * 5 + (tile,) + (P(),) * 6,
        out_specs=(act,) * 4 + (tile,) + (P(),) * 5,
        check_vma=False,
    )
```

```python
import functools
import math

import jax
import jax.numpy as jnp
from jax import lax
from jax.experimental import pallas as pl
from jax.experimental.pallas import tpu as pltpu
from jax.sharding import PartitionSpec as P

norm_eps = 1e-05
masked_score = -1e9
HS = 48
LOG2E = 1.4426950408889634
LN2 = 0.6931471805599453
f32 = jnp.float32
bf16 = jnp.bfloat16
V = pltpu.VMEM
VMEM_LIMIT = 62 << 20


def spec():
    return pl.BlockSpec(memory_space=V)


def dot(a, b, ca=1, cb=0):
    return lax.dot_general(a, b, (((ca,), (cb,)), ((), ())), preferred_element_type=f32)


def norm_rows(x):
    mean = jnp.mean(x, axis=-1, keepdims=True)
    centred = x - mean
    var = jnp.mean(centred * centred, axis=-1, keepdims=True)
    inv = lax.rsqrt(var + norm_eps)
    return centred * inv, inv


def position():
    seq, samp = lax.axis_index("seq"), lax.axis_index("samp")
    return {
        "seq": seq,
        "samp": samp,
        "core": lax.rem(seq, 2),
        "z": lax.rem(seq // 2, 4),
        "x": lax.rem(samp, 4),
        "y": (samp // 4) * 2 + seq // 8,
    }


def along(pos, axis, step):
    new = dict(pos)
    new[axis] = lax.rem(pos[axis] + step, 4)
    return ((lax.rem(new["y"], 2)) * 8 + new["z"] * 2 + pos["core"], (new["y"] // 2) * 4 + new["x"])


def seq_peer(pos, step):
    return (lax.rem(pos["seq"] + step, 16), pos["samp"])


def samp_peer(pos, step):
    return (pos["seq"], lax.rem(pos["samp"] + step, 8))


def core_peer(pos):
    return (pos["seq"] + 1 - 2 * pos["core"], pos["samp"])


def remote(src, dst, ss, rs, dev):
    return pltpu.make_async_remote_copy(
        src_ref=src, dst_ref=dst, send_sem=ss, recv_sem=rs, device_id=dev, device_id_type=pl.DeviceIdType.MESH
    )


def greet(devices):
    barrier = pltpu.get_barrier_semaphore()
    for d in devices:
        pl.semaphore_signal(barrier, inc=1, device_id=d, device_id_type=pl.DeviceIdType.MESH)
    return lambda: pl.semaphore_wait(barrier, len(devices))


AXES = (("x", "y", "z"), ("y", "z", "x"), ("z", "x", "y"))


def block_kernel(tok, scale, shift, og, dout, pbias, mask, wq, wk, wv, wg, wo,
                 dtok, dscale, dshift, dog, F, dpair,
                 send, recv, back, BR, BF, bm, acc, xs, kn, vn, dkv, sig, dgated, adT, dproj,
                 G, R0, R1, B1, R2, R3, DBS, DB, SB, RP,
                 bas, bar, bgs, bgr, q1s, q1r, q2s, q2r, o1s, o1r, o2s, o2r,
                 s0s, s0r, s1s, s1r, s2s, s2r, s3s, s3r, g2s, g2r, g1s, g1r, gcs, gcr, dbs, dbr, prs, prr):
    T = 1024
    R = 256
    pos = position()
    me = pos["seq"]
    core = pos["core"]
    other = 1 - core
    mine = [core * 3 + p for p in range(3)]
    peers = [seq_peer(pos, k) for k in range(1, 16)] + [samp_peer(pos, k) for k in range(1, 8)]
    far_y = along(pos, "y", jnp.where(lax.rem(pos["y"], 2) == 0, 3, 1))
    arrived = greet(peers + [far_y])

    normed, inv = norm_rows(tok[...].astype(f32))
    adapted = (normed * scale[...].astype(f32) + shift[...].astype(f32)).astype(bf16)

    arrived()
    bias_in = []
    for k in range(1, 16):
        dev = seq_peer(pos, k)
        c = remote(pbias.at[dev[0]], BR.at[me], bas.at[k], bar.at[k], dev)
        c.start()
        bias_in.append(c)
    BR[me] = pbias[me]

    def put_heads(t, val):
        vt = jnp.transpose(val.astype(bf16))
        for h in range(16):
            send[h, HS * t : HS * t + HS, :] = vt[HS * h : HS * h + HS, :]

    def send_heads(first, ss, rs):
        cs = []
        rows = slice(first, first + 96)
        for k in range(1, 16):
            dev = seq_peer(pos, k)
            c = remote(send.at[dev[0], rows], recv.at[me, rows], ss.at[k], rs.at[k], dev)
            c.start()
            cs.append(c)
        recv[me, rows, :] = send[me, rows, :]
        return cs

    put_heads(0, dot(adapted, wq[...]) * (LOG2E / math.sqrt(HS)))
    put_heads(1, dot(adapted, wk[...]))
    qk_copies = send_heads(0, q1s, q1r)

    for c in bias_in:
        c.wait()
    bias_out = []
    for k in range(1, 8):
        c = remote(BR, BF.at[pos["samp"]], bgs.at[k], bgr.at[k], samp_peer(pos, k))
        c.start()
        bias_out.append(c)
    BF[pos["samp"]] = BR[...]

    put_heads(2, dot(adapted, wv[...]))
    gate = jax.nn.sigmoid(dot(adapted, wg[...]))
    sig[...] = gate
    dp = (dout[...].astype(f32) * og[...].astype(f32)).astype(bf16)
    dproj[...] = dp
    dg = dot(dp, wo[...], 1, 1)
    dgated[...] = dg
    put_heads(3, dg * gate)
    va_copies = send_heads(96, q2s, q2r)
    adT[...] = jnp.transpose(adapted)

    live = mask[...] > 0
    livef = live.astype(f32)
    for c in qk_copies + va_copies:
        c.wait()
    for s in range(4):
        p, half = s // 2, s % 2
        lanes = slice(128 * p + 64 * half, 128 * p + 64 * half + 64)
        for b in range(8):
            xs[s, :, 128 * b : 128 * b + 128] = jnp.concatenate(
                [recv[2 * b, :, lanes], recv[2 * b + 1, :, lanes]], axis=1
            )
        km = jnp.where(live, xs[s, 48:96, :].astype(f32), 0.0).astype(bf16)
        xs[s, 48:96, :] = km
        kn[s] = jnp.transpose(km)
        vn[s] = jnp.transpose(xs[s, 96:144, :])
        dkv[s] = jnp.zeros((96, T), f32)

    for c in bias_out:
        c.wait()

    def prep(i, c):
        rows = pl.ds(pl.multiple_of(i * 128, 128), 128)
        for b in range(8):
            sl = slice(128 * b, 128 * b + 128)
            tile = BF[b, pl.ds(2 * i, 2)].reshape(128, 128)
            bm[rows, sl] = jnp.where(live[:, sl], tile.astype(f32) * LOG2E, masked_score)
        return c

    lax.fori_loop(0, T // 128, prep, 0)

    def block(ib, carry):
        i = lax.rem(me // 4 + 1 + ib, 4)
        rows = pl.ds(pl.multiple_of(i * R, R), R)

        def sample(s, c2):
            kT = xs[s, 48:96, :]
            vT = xs[s, 96:144, :]
            qT = xs[s, 0:48, rows]
            S = dot(jnp.transpose(qT), kT) + bm[rows, :]
            m = jnp.max(S, axis=1, keepdims=True)
            e = jnp.exp2(S - m)
            rinv = 1.0 / jnp.sum(e, axis=1, keepdims=True)
            eb = e.astype(bf16)
            att = dot(eb, vn[s]) * rinv
            da = (jnp.transpose(xs[s, 144:192, rows]).astype(f32) * rinv).astype(bf16)
            delta = jnp.sum(da.astype(f32) * att, axis=1, keepdims=True)
            hi = delta.astype(bf16)
            lo = (delta - hi.astype(f32)).astype(bf16)
            daext = jnp.concatenate([da, -hi, -lo, jnp.zeros((R, 14), bf16)], axis=1)
            vext = jnp.concatenate([vT, jnp.ones((16, T), bf16)], axis=0)
            dS = e * dot(daext, vext)
            dSb = dS.astype(bf16)

            @pl.when(s == 0)
            def _():
                acc[...] = dS

            @pl.when(s > 0)
            def _():
                acc[...] += dS

            dq = dot(dSb, kn[s]) * (1.0 / math.sqrt(HS))
            dkv[s, 0:48, :] += dot(qT, dSb)
            dkv[s, 48:96, :] += dot(jnp.transpose(da), eb)
            both = jnp.transpose(jnp.concatenate([att, dq], axis=1).astype(bf16))
            xs[s, 0:48, rows] = both[0:48]
            xs[s, 144:192, rows] = both[48:96]
            return c2

        lax.fori_loop(0, 4, sample, 0)

        for r in range(4):
            dev = 4 * i + r
            lanes = pl.ds(pl.multiple_of(i * R + 128 * (r // 2), 128), 128)
            hl = slice(64 * (r % 2), 64 * (r % 2) + 64)
            tiles = [xs[s, :, lanes] for s in range(4)]
            for p in range(2):
                both = jnp.concatenate([tiles[2 * p][:, hl], tiles[2 * p + 1][:, hl]], axis=1)
                send[dev, 0:48, 128 * p : 128 * p + 128] = both[0:48]
                send[dev, 48:96, 128 * p : 128 * p + 128] = both[144:192]

            @pl.when(dev != me)
            def _():
                k = lax.rem(dev - me + 16, 16)
                remote(send.at[dev, 0:96], back.at[me, 0:96], o1s.at[k], o1r.at[k], (dev, pos["samp"])).start()

            @pl.when(dev == me)
            def _():
                back[me, 0:96, :] = send[me, 0:96, :]

        for b in range(8):
            sl = slice(128 * b, 128 * b + 128)
            DBS[b, rows, :] = (acc[:, sl] * livef[:, sl]).astype(bf16)
        for k in range(1, 8):
            dev = samp_peer(pos, k)
            remote(DBS.at[dev[1], rows], DB.at[k - 1, rows], dbs.at[i, k], dbr.at[i, k], dev).start()
        return carry

    lax.fori_loop(0, T // R, block, 0)

    for s in range(4):
        xs[s, 48:96, :] = (dkv[s, 0:48, :] * (livef * LN2)).astype(bf16)
        xs[s, 96:144, :] = dkv[s, 48:96, :].astype(bf16)
    for b in range(8):
        for half in range(2):
            lanes = slice(128 * b + 64 * half, 128 * b + 64 * half + 64)
            for p in range(2):
                send[2 * b + half, 96:192, 128 * p : 128 * p + 128] = jnp.concatenate(
                    [xs[2 * p, 48:144, lanes], xs[2 * p + 1, 48:144, lanes]], axis=1
                )
    home2 = []
    for k in range(1, 16):
        dev = seq_peer(pos, k)
        c = remote(send.at[dev[0], 96:192], back.at[me, 96:192], o2s.at[k], o2r.at[k], dev)
        c.start()
        home2.append(c)
    back[me, 96:192, :] = send[me, 96:192, :]

    def get(t):
        xT = jnp.concatenate([back[h, HS * t : HS * t + HS, :] for h in range(16)], axis=0)
        return jnp.transpose(xT)

    first = []

    def put(m, val):
        rows = slice(768 * m, 768 * m + 768)
        for j in range(6):
            G[j, rows, :] = val[:, 128 * j : 128 * j + 128].astype(bf16)
        for p in range(3):
            c = remote(G.at[other * 3 + p, rows], R0.at[p, rows], s0s.at[p, m], s0r.at[p, m], core_peer(pos))
            c.start()
            first.append(c)

    for k in range(1, 16):
        remote(send.at[0, 0:96], back.at[0, 0:96], o1s.at[k], o1r.at[k], seq_peer(pos, k)).wait()

    cot = dout[...].astype(f32)
    gs = sig[...]
    att = get(0).astype(f32)
    gated = (gs * att).astype(bf16)
    put(4, dot(gated, dproj[...], 0, 0))
    dgl = (dgated[...] * att * gs * (1.0 - gs)).astype(bf16)
    put(3, dot(adT[...], dgl))
    dxs = [get(1)]
    put(0, dot(adT[...], dxs[0]))
    for c in home2:
        c.wait()
    for m in (1, 2):
        dxs.append(get(m + 1))
        put(m, dot(adT[...], dxs[m]))

    for c in first:
        c.wait()

    def add0(p):
        def body(i, carry):
            rows = pl.ds(pl.multiple_of(i * 960, 960), 960)
            j = mine[p]
            G[j, rows, :] = (G[j, rows, :].astype(f32) + R0[p, rows, :].astype(f32)).astype(bf16)
            return carry
        lax.fori_loop(0, 4, body, 0)

    def quarter(i):
        return pl.ds(pl.multiple_of(i * 960, 960), 960)

    def piece(i):
        return pl.ds(pl.multiple_of(i * 240, 240), 240)

    c1 = []
    for p in range(3):
        add0(p)
        a1 = AXES[p][0]
        for k in range(1, 4):
            t = lax.rem(pos[a1] + k, 4)
            c = remote(G.at[mine[p], quarter(t)], R1.at[p, k - 1], s1s.at[p, k - 1], s1r.at[p, k - 1], along(pos, a1, k))
            c.start()
            c1.append(c)

    normed, inv = norm_rows(tok[...].astype(f32))
    dog[...] = (cot * dot(gated, wo[...])).astype(bf16)
    d_ad = dot(dgl, wg[...], 1, 1)
    for m, w in enumerate((wq, wk, wv)):
        d_ad = d_ad + dot(dxs[m], w[...], 1, 1)
    dshift[...] = d_ad.astype(bf16)
    dscale[...] = (d_ad * normed).astype(bf16)
    dn = d_ad * scale[...].astype(f32)
    m1 = jnp.mean(dn, axis=-1, keepdims=True)
    m2 = jnp.mean(dn * normed, axis=-1, keepdims=True)
    dtok[...] = (cot + inv * (dn - m1 - normed * m2)).astype(bf16)

    c2 = []
    for p in range(3):
        for c in c1[3 * p : 3 * p + 3]:
            c.wait()
        a1, a2 = AXES[p][0], AXES[p][1]
        own = quarter(pos[a1])
        B1[p] = (G[mine[p], own, :].astype(f32) + R1[p, 0].astype(f32) + R1[p, 1].astype(f32) + R1[p, 2].astype(f32)).astype(bf16)
        for k in range(1, 4):
            t = lax.rem(pos[a2] + k, 4)
            c = remote(B1.at[p, piece(t)], R2.at[p, k - 1], s2s.at[p, k - 1], s2r.at[p, k - 1], along(pos, a2, k))
            c.start()
            c2.append(c)

    c3 = []
    for p in range(3):
        for c in c2[3 * p : 3 * p + 3]:
            c.wait()
        a2, a3 = AXES[p][1], AXES[p][2]
        at = pos[a3]
        R3[p, at] = (B1[p, piece(pos[a2]), :].astype(f32) + R2[p, 0].astype(f32) + R2[p, 1].astype(f32) + R2[p, 2].astype(f32)).astype(bf16)
        for k in range(1, 4):
            c = remote(R3.at[p, at], R3.at[p, at], s3s.at[p, k - 1], s3r.at[p, k - 1], along(pos, a3, k))
            c.start()
            c3.append(c)

    cg2 = []
    for p in range(3):
        for c in c3[3 * p : 3 * p + 3]:
            c.wait()
        a1, a2 = AXES[p][0], AXES[p][1]
        rows = pl.ds(pl.multiple_of(pos[a1] * 960 + pos[a2] * 240, 240), 240)
        F[mine[p], rows, :] = (R3[p, 0].astype(f32) + R3[p, 1].astype(f32) + R3[p, 2].astype(f32) + R3[p, 3].astype(f32)).astype(bf16)
        for k in range(1, 4):
            c = remote(F.at[mine[p], rows], F.at[mine[p], rows], g2s.at[p, k - 1], g2r.at[p, k - 1], along(pos, a2, k))
            c.start()
            cg2.append(c)

    cg1 = []
    cgc = []

    def to_core(p, k, t):
        c = remote(F.at[mine[p], quarter(t)], F.at[mine[p], quarter(t)], gcs.at[p, k], gcr.at[p, k], core_peer(pos))
        c.start()
        cgc.append(c)

    for p in range(3):
        for c in cg2[3 * p : 3 * p + 3]:
            c.wait()
        a1 = AXES[p][0]
        own = quarter(pos[a1])
        for k in range(1, 4):
            c = remote(F.at[mine[p], own], F.at[mine[p], own], g1s.at[p, k - 1], g1r.at[p, k - 1], along(pos, a1, k))
            c.start()
            cg1.append(c)
        to_core(p, 0, pos[a1])

    for i in range(4):
        for k in range(1, 8):
            rows = slice(256 * i, 256 * i + 256)
            remote(DBS.at[0, rows], DB.at[k - 1, rows], dbs.at[i, k], dbr.at[i, k], samp_peer(pos, k)).wait()
    def sum_bias(i, carry):
        rows = pl.ds(pl.multiple_of(i * 128, 128), 128)
        tot = DBS[pos["samp"], rows, :].astype(f32)
        for k in range(7):
            tot = tot + DB[k, rows, :].astype(f32)
        SB[rows, :] = tot.astype(bf16)
        return carry
    lax.fori_loop(0, 8, sum_bias, 0)
    pr = []
    for k in range(1, 16):
        dev = seq_peer(pos, k)
        rows = pl.ds(pl.multiple_of(dev[0] * 64, 64), 64)
        c = remote(SB.at[rows], RP.at[pos["seq"]], prs.at[k - 1], prr.at[k - 1], dev)
        c.start()
        pr.append(c)
    RP[pos["seq"]] = SB[pl.ds(pl.multiple_of(pos["seq"] * 64, 64), 64), :]

    for p in range(3):
        for k in range(1, 4):
            cg1[3 * p + k - 1].wait()
            to_core(p, k, lax.rem(pos[AXES[p][0]] + 4 - k, 4))
    for c in pr:
        c.wait()
    dpair[...] = RP[...].astype(f32)
    for c in cgc:
        c.wait()


def widen_kernel(F, *outs):
    for m in range(5):
        for j in range(6):
            outs[m][:, 128 * j : 128 * j + 128] = F[j, m].astype(f32)


def sds(shape, dtype):
    return jax.ShapeDtypeStruct(shape, dtype)


def on_device(tokens, ada_scale, ada_shift, out_gate, d_out, pair_bias, key_mask,
              w_query, w_key, w_value, w_gate, w_output):
    dma = lambda *shape: pltpu.SemaphoreType.DMA(shape)
    rows = lambda a: a.reshape(256, 768)
    tok, scale, shift, og, cot = map(rows, (tokens, ada_scale, ada_shift, out_gate, d_out))
    heads = V((16, 192, 256), bf16)
    dtok, dscale, dshift, dog, F, d_pair = pl.pallas_call(
        block_kernel,
        out_shape=(sds((256, 768), bf16),) * 4 + (sds((6, 3840, 128), bf16), sds((16, 64, 128), f32)),
        in_specs=[spec()] * 12,
        out_specs=[spec()] * 6,
        scratch_shapes=[heads, heads, heads, V((16, 64, 128), bf16), V((8, 16, 64, 128), bf16), V((1024, 1024), f32),
                        V((256, 1024), f32), V((4, 192, 1024), bf16), V((4, 1024, 48), bf16), V((4, 1024, 48), bf16),
                        V((4, 96, 1024), f32), V((256, 768), f32), V((256, 768), f32), V((768, 256), bf16), V((256, 768), bf16),
                        V((6, 3840, 128), bf16), V((3, 3840, 128), bf16), V((3, 3, 960, 128), bf16), V((3, 960, 128), bf16),
                        V((3, 3, 240, 128), bf16), V((3, 4, 240, 128), bf16), V((8, 1024, 128), bf16), V((7, 1024, 128), bf16),
                        V((1024, 128), bf16), V((16, 64, 128), bf16)]
        + [dma(16)] * 2 + [dma(8)] * 2 + [dma(16)] * 8
        + [dma(3, 5)] * 2 + [dma(3, 3)] * 10 + [dma(3, 4)] * 2 + [dma(4, 8)] * 2 + [dma(15)] * 2,
        compiler_params=pltpu.CompilerParams(vmem_limit_bytes=VMEM_LIMIT, collective_id=2, has_side_effects=True),
        cost_estimate=pl.CostEstimate(flops=16 * 10**9, bytes_accessed=20 << 20, transcendentals=5 << 20),
    )(tok, scale, shift, og, cot, pair_bias, key_mask.reshape(1, 1024), w_query, w_key, w_value, w_gate, w_output)
    grads = pl.pallas_call(
        widen_kernel,
        grid=(6,),
        out_shape=(sds((768, 768), f32),) * 5,
        in_specs=[pl.BlockSpec((6, 5, 128, 128), lambda i: (0, 0, i, 0))],
        out_specs=[pl.BlockSpec((128, 768), lambda i: (i, 0))] * 5,
    )(F.reshape(6, 5, 768, 128))
    shaped = lambda a: a.reshape(4, 64, 768)
    return (shaped(dtok), shaped(dscale), shaped(dshift), shaped(dog), d_pair,
            grads[0], grads[1], grads[2], grads[3], grads[4])


def solution(mesh):
    act = P("samp", "seq", None)
    tile = P(None, "seq", "samp")
    return jax.shard_map(
        on_device,
        mesh=mesh,
        in_specs=(act,) * 5 + (tile,) + (P(),) * 6,
        out_specs=(act,) * 4 + (tile,) + (P(),) * 5,
        check_vma=False,
    )
```

```python
import functools
import math

import jax
import jax.numpy as jnp
from jax import lax
from jax.experimental import pallas as pl
from jax.experimental.pallas import tpu as pltpu
from jax.sharding import PartitionSpec as P

norm_eps = 1e-05
masked_score = -1e9
HS = 48
LOG2E = 1.4426950408889634
LN2 = 0.6931471805599453
f32 = jnp.float32
bf16 = jnp.bfloat16
V = pltpu.VMEM
VMEM_LIMIT = 62 << 20


def spec():
    return pl.BlockSpec(memory_space=V)


def dot(a, b, ca=1, cb=0):
    return lax.dot_general(a, b, (((ca,), (cb,)), ((), ())), preferred_element_type=f32)


def norm_rows(x):
    mean = jnp.mean(x, axis=-1, keepdims=True)
    centred = x - mean
    var = jnp.mean(centred * centred, axis=-1, keepdims=True)
    inv = lax.rsqrt(var + norm_eps)
    return centred * inv, inv


def position():
    seq, samp = lax.axis_index("seq"), lax.axis_index("samp")
    return {
        "seq": seq,
        "samp": samp,
        "core": lax.rem(seq, 2),
        "z": lax.rem(seq // 2, 4),
        "x": lax.rem(samp, 4),
        "y": (samp // 4) * 2 + seq // 8,
    }


def along(pos, axis, step):
    new = dict(pos)
    new[axis] = lax.rem(pos[axis] + step, 4)
    return ((lax.rem(new["y"], 2)) * 8 + new["z"] * 2 + pos["core"], (new["y"] // 2) * 4 + new["x"])


def seq_peer(pos, step):
    return (lax.rem(pos["seq"] + step, 16), pos["samp"])


def samp_peer(pos, step):
    return (pos["seq"], lax.rem(pos["samp"] + step, 8))


def core_peer(pos):
    return (pos["seq"] + 1 - 2 * pos["core"], pos["samp"])


def remote(src, dst, ss, rs, dev):
    return pltpu.make_async_remote_copy(
        src_ref=src, dst_ref=dst, send_sem=ss, recv_sem=rs, device_id=dev, device_id_type=pl.DeviceIdType.MESH
    )


def greet(devices):
    barrier = pltpu.get_barrier_semaphore()
    for d in devices:
        pl.semaphore_signal(barrier, inc=1, device_id=d, device_id_type=pl.DeviceIdType.MESH)
    return lambda: pl.semaphore_wait(barrier, len(devices))


AXES = (("x", "y", "z"), ("y", "z", "x"), ("z", "x", "y"))


def block_kernel(tok, scale, shift, og, dout, pbias, mask, wq, wk, wv, wg, wo,
                 dtok, dscale, dshift, dog, F, RP,
                 send, recv, back, BR, BF, bm, acc, xs, kn, vn, dkv, sig, dgated, adT, dproj,
                 G, R0, R1a, B1a, R2a, R3a, R1b, B1b, R2b, R3b, DBS, DB, SB, DY,
                 bas, bar, bxs, bxr, bys, byr, bfs, bfr, q1s, q1r, q2s, q2r, o1s, o1r, o2s, o2r,
                 s0s, s0r, s1s, s1r, s2s, s2r, s3s, s3r, g2s, g2r, g1s, g1r, gcs, gcr, dbs, dbr, dys, dyr, prs, prr):
    T = 1024
    R = 256
    pos = position()
    me = pos["seq"]
    samp = pos["samp"]
    core = pos["core"]
    other = 1 - core
    mine = [core * 3 + p for p in range(3)]
    peers = [seq_peer(pos, k) for k in range(1, 16)] + [samp_peer(pos, k) for k in range(1, 8)]
    far_y = along(pos, "y", jnp.where(lax.rem(pos["y"], 2) == 0, 3, 1))
    arrived = greet(peers + [far_y])

    normed, inv = norm_rows(tok[...].astype(f32))
    adapted = (normed * scale[...].astype(f32) + shift[...].astype(f32)).astype(bf16)
    dp = (dout[...].astype(f32) * og[...].astype(f32)).astype(bf16)
    dproj[...] = dp

    arrived()
    bias_in = []
    for k in range(1, 16):
        dev = seq_peer(pos, k)
        c = remote(pbias.at[dev[0]], BR.at[me], bas.at[k], bar.at[k], dev)
        c.start()
        bias_in.append(c)
    BR[me] = pbias[me]

    def put_heads(p, t, val):
        vt = jnp.transpose(val.astype(bf16))
        for h in range(16):
            send[p, h, HS * t : HS * t + HS, :] = vt[HS * h : HS * h + HS, :]

    def send_heads(p, first, ss, rs):
        cs = []
        rows = slice(first, first + 96)
        for k in range(1, 16):
            dev = seq_peer(pos, k)
            c = remote(send.at[p, dev[0], rows], recv.at[p, me, rows], ss.at[p, k], rs.at[p, k], dev)
            c.start()
            cs.append(c)
        recv[p, me, rows, :] = send[p, me, rows, :]
        return cs

    def chunk(ib):
        i = lax.rem(me // 4 + 1 + ib, 4)
        return i, pl.ds(4 * i, 4)

    ad = adapted[0:128]
    put_heads(0, 0, dot(ad, wq[...]) * (LOG2E / math.sqrt(HS)))
    put_heads(0, 1, dot(ad, wk[...]))
    head_copies = [send_heads(0, 0, q1s, q1r), None]

    for c in bias_in:
        c.wait()
    by = []
    for ib in range(4):
        i, cr = chunk(ib)
        c = remote(BR.at[cr], BF.at[samp, cr], bys.at[ib], byr.at[ib], samp_peer(pos, 4))
        c.start()
        by.append(c)

    def bias_on(ib):
        i, cr = chunk(ib)
        for k in range(1, 4):
            remote(BR.at[cr], BF.at[samp, cr], bxs.at[ib, k], bxr.at[ib, k], along(pos, "x", k)).start()

    bias_on(0)
    bias_on(1)
    BF[samp] = BR[...]

    def gate_part(p, r):
        gate = jax.nn.sigmoid(dot(adapted[r], wg[...]))
        sig[r, :] = gate
        dg = dot(dp[r], wo[...], 1, 1)
        dgated[r, :] = dg
        put_heads(p, 2, dot(adapted[r], wv[...]))
        put_heads(p, 3, dg * gate)
        return send_heads(p, 96, q2s, q2r)

    head_copies[0] += gate_part(0, slice(0, 128))

    twin = lax.rem(samp + 4, 8)
    for ib in range(4):
        if ib > 1:
            bias_on(ib)
        by[ib].wait()
        i, cr = chunk(ib)
        for k in range(1, 4):
            remote(BF.at[twin, cr], BF.at[twin, cr], bfs.at[ib, k], bfr.at[ib, k], along(pos, "x", k)).start()

    ad = adapted[128:256]
    put_heads(1, 0, dot(ad, wq[...]) * (LOG2E / math.sqrt(HS)))
    put_heads(1, 1, dot(ad, wk[...]))
    head_copies[1] = send_heads(1, 0, q1s, q1r)
    head_copies[1] += gate_part(1, slice(128, 256))
    adT[...] = jnp.transpose(adapted)

    live = mask[...] > 0
    livef = live.astype(f32)
    home2 = []

    for p in range(2):
        for c in head_copies[p]:
            c.wait()
        for half in range(2):
            s = 2 * p + half
            lanes = slice(64 * half, 64 * half + 64)
            for b in range(8):
                xs[s, :, 128 * b : 128 * b + 128] = jnp.concatenate(
                    [recv[p, 2 * b, :, lanes], recv[p, 2 * b + 1, :, lanes]], axis=1
                )
            km = jnp.where(live, xs[s, 48:96, :].astype(f32), 0.0).astype(bf16)
            xs[s, 48:96, :] = km
            kn[s] = jnp.transpose(km)
            vn[s] = jnp.transpose(xs[s, 96:144, :])
            dkv[half] = jnp.zeros((96, T), f32)

        def block(ib, carry):
            i, cr = chunk(ib)
            rows = pl.ds(pl.multiple_of(i * R, R), R)

            if p == 0:
                for k in range(1, 4):
                    remote(BR.at[cr], BF.at[samp, cr], bxs.at[ib, k], bxr.at[ib, k], along(pos, "x", k)).wait()
                    remote(BF.at[twin, cr], BF.at[twin, cr], bfs.at[ib, k], bfr.at[ib, k], along(pos, "x", k)).wait()
                for b in range(8):
                    sl = slice(128 * b, 128 * b + 128)
                    tile = BF[b, cr].reshape(R, 128)
                    bm[rows, sl] = jnp.where(live[:, sl], tile.astype(f32) * LOG2E, masked_score)

            def sample(half, c2):
                s = 2 * p + half
                kT = xs[s, 48:96, :]
                vT = xs[s, 96:144, :]
                qT = xs[s, 0:48, rows]
                S = dot(jnp.transpose(qT), kT) + bm[rows, :]
                m = jnp.max(S, axis=1, keepdims=True)
                e = jnp.exp2(S - m)
                rinv = 1.0 / jnp.sum(e, axis=1, keepdims=True)
                eb = e.astype(bf16)
                att = dot(eb, vn[s]) * rinv
                da = (jnp.transpose(xs[s, 144:192, rows]).astype(f32) * rinv).astype(bf16)
                delta = jnp.sum(da.astype(f32) * att, axis=1, keepdims=True)
                hi = delta.astype(bf16)
                lo = (delta - hi.astype(f32)).astype(bf16)
                daext = jnp.concatenate([da, -hi, -lo, jnp.zeros((R, 14), bf16)], axis=1)
                vext = jnp.concatenate([vT, jnp.ones((16, T), bf16)], axis=0)
                dS = e * dot(daext, vext)
                dSb = dS.astype(bf16)
                if p == 0:

                    @pl.when(half == 0)
                    def _():
                        acc[rows, :] = dS

                    @pl.when(half > 0)
                    def _():
                        acc[rows, :] += dS

                else:
                    acc[rows, :] += dS
                dq = dot(dSb, kn[s]) * (1.0 / math.sqrt(HS))
                dkv[half, 0:48, :] += dot(qT, dSb)
                dkv[half, 48:96, :] += dot(jnp.transpose(da), eb)
                both = jnp.transpose(jnp.concatenate([att, dq], axis=1).astype(bf16))
                xs[s, 0:48, rows] = both[0:48]
                xs[s, 144:192, rows] = both[48:96]
                return c2

            lax.fori_loop(0, 2, sample, 0)

            for r in range(4):
                dev = 4 * i + r
                lanes = pl.ds(pl.multiple_of(i * R + 128 * (r // 2), 128), 128)
                hl = slice(64 * (r % 2), 64 * (r % 2) + 64)
                both = jnp.concatenate([xs[2 * p, :, lanes][:, hl], xs[2 * p + 1, :, lanes][:, hl]], axis=1)
                send[p, dev, 0:48, :] = both[0:48]
                send[p, dev, 48:96, :] = both[144:192]

                @pl.when(dev != me)
                def _():
                    k = lax.rem(dev - me + 16, 16)
                    remote(send.at[p, dev, 0:96], back.at[p, me, 0:96], o1s.at[p, k], o1r.at[p, k], (dev, samp)).start()

                @pl.when(dev == me)
                def _():
                    back[p, me, 0:96, :] = send[p, me, 0:96, :]

            if p == 1:
                for b in range(8):
                    sl = slice(128 * b, 128 * b + 128)
                    DBS[b, rows, :] = (acc[rows, sl] * livef[:, sl]).astype(bf16)
                for k in range(1, 4):
                    dev = along(pos, "x", k)
                    for y in range(2):
                        b = lax.rem(dev[1], 4) + 4 * y
                        remote(DBS.at[b, rows], DB.at[k - 1, y, rows], dbs.at[i, 2 * k + y], dbr.at[i, 2 * k + y], dev).start()
            return carry

        lax.fori_loop(0, T // R, block, 0)

        for half in range(2):
            xs[2 * p + half, 48:96, :] = (dkv[half, 0:48, :] * (livef * LN2)).astype(bf16)
            xs[2 * p + half, 96:144, :] = dkv[half, 48:96, :].astype(bf16)
        for b in range(8):
            for half in range(2):
                lanes = slice(128 * b + 64 * half, 128 * b + 64 * half + 64)
                send[p, 2 * b + half, 96:192, :] = jnp.concatenate(
                    [xs[2 * p, 48:144, lanes], xs[2 * p + 1, 48:144, lanes]], axis=1
                )
        for k in range(1, 16):
            dev = seq_peer(pos, k)
            c = remote(send.at[p, dev[0], 96:192], back.at[p, me, 96:192], o2s.at[p, k], o2r.at[p, k], dev)
            c.start()
            home2.append(c)
        back[p, me, 96:192, :] = send[p, me, 96:192, :]

    def get(t):
        return jnp.concatenate(
            [
                jnp.transpose(jnp.concatenate([back[p, h, HS * t : HS * t + HS, :] for h in range(16)], axis=0))
                for p in range(2)
            ],
            axis=0,
        )

    first = {}
    place = {4: 0, 3: 1, 0: 2, 1: 3, 2: 4}

    def put(m, val):
        at = place[m]
        rows = slice(768 * at, 768 * at + 768)
        for j in range(6):
            G[j, rows, :] = val[:, 128 * j : 128 * j + 128].astype(bf16)
        first[at] = []
        for p in range(3):
            c = remote(G.at[other * 3 + p, rows], R0.at[p, rows], s0s.at[p, at], s0r.at[p, at], core_peer(pos))
            c.start()
            first[at].append(c)

    groups = [(0, 2304, R1a, B1a, R2a, R3a), (2304, 1536, R1b, B1b, R2b, R3b)]
    flying = {}

    def quarter(g, i):
        base, n = groups[g][:2]
        return pl.ds(pl.multiple_of(base + i * (n // 4), 16), n // 4)

    def piece(g, i):
        n = groups[g][1] // 16
        return pl.ds(pl.multiple_of(i * n, 16), n)

    def ring(key, g, p, axis, ss, rs, ref):
        out = []
        for k in range(1, 4):
            src, dst = ref(k)
            c = remote(src, dst, ss.at[g, p, k], rs.at[g, p, k], along(pos, axis, k))
            c.start()
            out.append(c)
        flying[key, g, p] = out

    def land(key, g, p):
        for c in flying[key, g, p]:
            c.wait()

    def scatter1(g):
        base, n, R1 = groups[g][:3]
        for at in range(base // 768, (base + n) // 768):
            for c in first[at]:
                c.wait()
        for p in range(3):
            j = mine[p]
            a1 = AXES[p][0]

            def add(i, carry):
                rows = pl.ds(pl.multiple_of(base + i * 384, 384), 384)
                G[j, rows, :] = (G[j, rows, :].astype(f32) + R0[p, rows, :].astype(f32)).astype(bf16)
                return carry

            lax.fori_loop(0, n // 384, add, 0)
            ring("s1", g, p, a1, s1s, s1r, lambda k: (G.at[j, quarter(g, lax.rem(pos[a1] + k, 4))], R1.at[p, k - 1]))

    def scatter2(g):
        R1, B1, R2 = groups[g][2:5]
        for p in range(3):
            land("s1", g, p)
            a1, a2 = AXES[p][0], AXES[p][1]
            tot = G[mine[p], quarter(g, pos[a1]), :].astype(f32)
            for k in range(3):
                tot = tot + R1[p, k].astype(f32)
            B1[p] = tot.astype(bf16)
            ring("s2", g, p, a2, s2s, s2r, lambda k: (B1.at[p, piece(g, lax.rem(pos[a2] + k, 4))], R2.at[p, k - 1]))

    def exchange(g):
        B1, R2, R3 = groups[g][3:6]
        for p in range(3):
            land("s2", g, p)
            a2, a3 = AXES[p][1], AXES[p][2]
            tot = B1[p, piece(g, pos[a2]), :].astype(f32)
            for k in range(3):
                tot = tot + R2[p, k].astype(f32)
            at = pos[a3]
            R3[p, at] = tot.astype(bf16)
            ring("s3", g, p, a3, s3s, s3r, lambda k: (R3.at[p, at], R3.at[p, at]))

    def gather2(g):
        base, n = groups[g][:2]
        R3 = groups[g][5]
        for p in range(3):
            land("s3", g, p)
            a1, a2 = AXES[p][0], AXES[p][1]
            rows = pl.ds(pl.multiple_of(base + pos[a1] * (n // 4) + pos[a2] * (n // 16), 16), n // 16)
            F[mine[p], rows, :] = (
                R3[p, 0].astype(f32) + R3[p, 1].astype(f32) + R3[p, 2].astype(f32) + R3[p, 3].astype(f32)
            ).astype(bf16)
            ring("g2", g, p, a2, g2s, g2r, lambda k: (F.at[mine[p], rows], F.at[mine[p], rows]))

    cgc = []

    def to_core(g, p, k, t):
        part = F.at[mine[p], quarter(g, t)]
        c = remote(part, part, gcs.at[g, p, k], gcr.at[g, p, k], core_peer(pos))
        c.start()
        cgc.append(c)

    def gather1(g):
        for p in range(3):
            land("g2", g, p)
            a1 = AXES[p][0]
            part = F.at[mine[p], quarter(g, pos[a1])]
            ring("g1", g, p, a1, g1s, g1r, lambda k: (part, part))
            to_core(g, p, 0, pos[a1])

    def gather0(g):
        for p in range(3):
            for k in range(1, 4):
                flying["g1", g, p][k - 1].wait()
                to_core(g, p, k, lax.rem(pos[AXES[p][0]] + 4 - k, 4))

    for p in range(2):
        for k in range(1, 16):
            remote(send.at[p, 0, 0:96], back.at[p, 0, 0:96], o1s.at[p, k], o1r.at[p, k], seq_peer(pos, k)).wait()

    cot = dout[...].astype(f32)
    gs = sig[...]
    att = get(0).astype(f32)
    gated = (gs * att).astype(bf16)
    put(4, dot(gated, dproj[...], 0, 0))
    dgl = (dgated[...] * att * gs * (1.0 - gs)).astype(bf16)
    put(3, dot(adT[...], dgl))
    dxs = [get(1)]
    put(0, dot(adT[...], dxs[0]))
    scatter1(0)
    for c in home2:
        c.wait()
    for m in (1, 2):
        dxs.append(get(m + 1))
        put(m, dot(adT[...], dxs[m]))
    scatter1(1)

    normed, inv = norm_rows(tok[...].astype(f32))
    dog[...] = (cot * dot(gated, wo[...])).astype(bf16)
    d_ad = dot(dgl, wg[...], 1, 1)
    for m, w in enumerate((wq, wk, wv)):
        d_ad = d_ad + dot(dxs[m], w[...], 1, 1)
    dshift[...] = d_ad.astype(bf16)
    dscale[...] = (d_ad * normed).astype(bf16)
    dn = d_ad * scale[...].astype(f32)
    m1 = jnp.mean(dn, axis=-1, keepdims=True)
    m2 = jnp.mean(dn * normed, axis=-1, keepdims=True)
    dtok[...] = (cot + inv * (dn - m1 - normed * m2)).astype(bf16)

    scatter2(0)
    scatter2(1)

    for i in range(4):
        for k in range(1, 4):
            for y in range(2):
                rows = slice(256 * i, 256 * i + 256)
                remote(DBS.at[0, rows], DB.at[k - 1, y, rows], dbs.at[i, 2 * k + y], dbr.at[i, 2 * k + y], along(pos, "x", k)).wait()

    def sum_bias(i, carry):
        rows = pl.ds(pl.multiple_of(i * 128, 128), 128)
        for y in range(2):
            tot = DBS[pos["x"] + 4 * y, rows, :].astype(f32)
            for k in range(3):
                tot = tot + DB[k, y, rows, :].astype(f32)
            SB[y, rows, :] = tot.astype(bf16)
        return carry

    lax.fori_loop(0, 8, sum_bias, 0)
    yhi = samp // 4
    hand = remote(SB.at[1 - yhi], DY, dys.at[0], dyr.at[0], samp_peer(pos, 4))
    hand.start()

    exchange(0)
    exchange(1)
    gather2(0)
    gather2(1)
    gather1(0)
    gather1(1)

    hand.wait()

    def sum_half(i, carry):
        rows = pl.ds(pl.multiple_of(i * 128, 128), 128)
        SB[yhi, rows, :] = (SB[yhi, rows, :].astype(f32) + DY[rows, :].astype(f32)).astype(bf16)
        return carry

    lax.fori_loop(0, 8, sum_half, 0)
    pr = []
    for k in range(1, 16):
        dev = seq_peer(pos, k)
        rows = pl.ds(pl.multiple_of(dev[0] * 64, 64), 64)
        c = remote(SB.at[yhi, rows], RP.at[me], prs.at[k - 1], prr.at[k - 1], dev)
        c.start()
        pr.append(c)
    RP[me] = SB[yhi, pl.ds(pl.multiple_of(me * 64, 64), 64), :]

    gather0(0)
    gather0(1)
    for c in pr + cgc:
        c.wait()


def widen_kernel(F, RP, *refs):
    acts, outs = refs[:4], refs[4:]
    for i in range(4):
        outs[i][...] = acts[i][...]
    outs[4][...] = RP[...].astype(f32)
    for m, at in ((0, 2), (1, 3), (2, 4), (3, 1), (4, 0)):
        for j in range(6):
            outs[5 + m][:, 128 * j : 128 * j + 128] = F[j, at].astype(f32)


def sds(shape, dtype):
    return jax.ShapeDtypeStruct(shape, dtype)


def on_device(tokens, ada_scale, ada_shift, out_gate, d_out, pair_bias, key_mask,
              w_query, w_key, w_value, w_gate, w_output):
    dma = lambda *shape: pltpu.SemaphoreType.DMA(shape)
    rows = lambda a: a.reshape(256, 768)
    tok, scale, shift, og, cot = map(rows, (tokens, ada_scale, ada_shift, out_gate, d_out))
    heads = V((2, 16, 192, 128), bf16)
    dtok, dscale, dshift, dog, F, RP = pl.pallas_call(
        block_kernel,
        out_shape=(sds((256, 768), bf16),) * 4 + (sds((6, 3840, 128), bf16), sds((16, 64, 128), bf16)),
        in_specs=[spec()] * 12,
        out_specs=[spec()] * 6,
        scratch_shapes=[heads, heads, heads, V((16, 64, 128), bf16), V((8, 16, 64, 128), bf16), V((1024, 1024), f32),
                        V((1024, 1024), f32), V((4, 192, 1024), bf16), V((4, 1024, 48), bf16), V((4, 1024, 48), bf16),
                        V((2, 96, 1024), f32), V((256, 768), f32), V((256, 768), f32), V((768, 256), bf16), V((256, 768), bf16),
                        V((6, 3840, 128), bf16), V((3, 3840, 128), bf16)]
        + [V(shape, bf16) for q in (576, 384)
           for shape in ((3, 3, q, 128), (3, q, 128), (3, 3, q // 4, 128), (3, 4, q // 4, 128))]
        + [V((8, 1024, 128), bf16), V((3, 2, 1024, 128), bf16), V((2, 1024, 128), bf16), V((1024, 128), bf16)]
        + [dma(16)] * 2 + [dma(4, 4)] * 2 + [dma(4)] * 2 + [dma(4, 4)] * 2 + [dma(2, 16)] * 8
        + [dma(3, 5)] * 2 + [dma(2, 3, 4)] * 12 + [dma(4, 8)] * 2 + [dma(1)] * 2 + [dma(15)] * 2,
        compiler_params=pltpu.CompilerParams(vmem_limit_bytes=VMEM_LIMIT, collective_id=2, has_side_effects=True),
        cost_estimate=pl.CostEstimate(flops=16 * 10**9, bytes_accessed=20 << 20, transcendentals=5 << 20),
    )(tok, scale, shift, og, cot, pair_bias, key_mask.reshape(1, 1024), w_query, w_key, w_value, w_gate, w_output)
    act = pl.BlockSpec((32, 768), lambda i: (i, 0))
    tile = pl.BlockSpec((2, 64, 128), lambda i: (i, 0, 0))
    outs = pl.pallas_call(
        widen_kernel,
        grid=(8,),
        out_shape=(sds((256, 768), bf16),) * 4 + (sds((16, 64, 128), f32),) + (sds((768, 768), f32),) * 5,
        in_specs=[pl.BlockSpec((6, 5, 96, 128), lambda i: (0, 0, i, 0)), tile] + [act] * 4,
        out_specs=[act] * 4 + [tile] + [pl.BlockSpec((96, 768), lambda i: (i, 0))] * 5,
    )(F.reshape(6, 5, 768, 128), RP, dtok, dscale, dshift, dog)
    shaped = lambda a: a.reshape(4, 64, 768)
    return tuple(map(shaped, outs[:4])) + tuple(outs[4:])


def solution(mesh):
    act = P("samp", "seq", None)
    tile = P(None, "seq", "samp")
    return jax.shard_map(
        on_device,
        mesh=mesh,
        in_specs=(act,) * 5 + (tile,) + (P(),) * 6,
        out_specs=(act,) * 4 + (tile,) + (P(),) * 5,
        check_vma=False,
    )
```

```python
import functools
import math

import jax
import jax.numpy as jnp
from jax import lax
from jax.experimental import pallas as pl
from jax.experimental.pallas import tpu as pltpu
from jax.sharding import PartitionSpec as P

norm_eps = 1e-05
masked_score = -1e9
HS = 48
LOG2E = 1.4426950408889634
LN2 = 0.6931471805599453
f32 = jnp.float32
bf16 = jnp.bfloat16
V = pltpu.VMEM
VMEM_LIMIT = 62 << 20


def spec():
    return pl.BlockSpec(memory_space=V)


def dot(a, b, ca=1, cb=0):
    return lax.dot_general(a, b, (((ca,), (cb,)), ((), ())), preferred_element_type=f32)


def norm_rows(x):
    mean = jnp.mean(x, axis=-1, keepdims=True)
    centred = x - mean
    var = jnp.mean(centred * centred, axis=-1, keepdims=True)
    inv = lax.rsqrt(var + norm_eps)
    return centred * inv, inv


def position():
    seq, samp = lax.axis_index("seq"), lax.axis_index("samp")
    return {
        "seq": seq,
        "samp": samp,
        "core": lax.rem(seq, 2),
        "z": lax.rem(seq // 2, 4),
        "x": lax.rem(samp, 4),
        "y": (samp // 4) * 2 + seq // 8,
    }


def along(pos, axis, step):
    new = dict(pos)
    new[axis] = lax.rem(pos[axis] + step, 4)
    return ((lax.rem(new["y"], 2)) * 8 + new["z"] * 2 + pos["core"], (new["y"] // 2) * 4 + new["x"])


def seq_peer(pos, step):
    return (lax.rem(pos["seq"] + step, 16), pos["samp"])


def samp_peer(pos, step):
    return (pos["seq"], lax.rem(pos["samp"] + step, 8))


def core_peer(pos):
    return (pos["seq"] + 1 - 2 * pos["core"], pos["samp"])


def remote(src, dst, ss, rs, dev):
    return pltpu.make_async_remote_copy(
        src_ref=src, dst_ref=dst, send_sem=ss, recv_sem=rs, device_id=dev, device_id_type=pl.DeviceIdType.MESH
    )


def greet(devices):
    barrier = pltpu.get_barrier_semaphore()
    for d in devices:
        pl.semaphore_signal(barrier, inc=1, device_id=d, device_id_type=pl.DeviceIdType.MESH)
    return lambda: pl.semaphore_wait(barrier, len(devices))


AXES = (("x", "y", "z"), ("y", "z", "x"), ("z", "x", "y"))


def block_kernel(tok, scale, shift, og, dout, pbias, mask, wq, wk, wv, wg, wo,
                 dtok, dscale, dshift, dog, F, RP,
                 send, recv, back, BR, bm, acc, xs, dkv, sig, dgated, adT, dproj,
                 G, R0, R1a, B1a, R2a, R3a, R1b, B1b, R2b, R3b, DBS, DB, SB, DY,
                 bas, bar, bxs, bxr, bys, byr, bfs, bfr, q1s, q1r, o1s, o1r, o2s, o2r,
                 s0s, s0r, s1s, s1r, s2s, s2r, s3s, s3r, g2s, g2r, g1s, g1r, gcs, gcr, dbs, dbr, dys, dyr, prs, prr):
    T = 1024
    R = 512
    pos = position()
    me = pos["seq"]
    samp = pos["samp"]
    core = pos["core"]
    other = 1 - core
    mine = [core * 3 + p for p in range(3)]
    peers = [seq_peer(pos, k) for k in range(1, 16)] + [samp_peer(pos, k) for k in range(1, 8)]
    far_y = along(pos, "y", jnp.where(lax.rem(pos["y"], 2) == 0, 3, 1))
    arrived = greet(peers + [far_y])

    normed, inv = norm_rows(tok[...].astype(f32))
    adapted = (normed * scale[...].astype(f32) + shift[...].astype(f32)).astype(bf16)
    dp = (dout[...].astype(f32) * og[...].astype(f32)).astype(bf16)
    dproj[...] = dp

    arrived()
    bias_in = []
    for k in range(1, 16):
        dev = seq_peer(pos, k)
        c = remote(pbias.at[dev[0]], BR.at[pl.ds(pl.multiple_of(me * 64, 64), 64)], bas.at[k], bar.at[k], dev)
        c.start()
        bias_in.append(c)
    BR[pl.ds(pl.multiple_of(me * 64, 64), 64), :] = pbias[me]

    def put_heads(p, t, first, second):
        first, second = first.astype(bf16), second.astype(bf16)
        for half in range(2):
            r = slice(64 * half, 64 * half + 64)
            vt = jnp.transpose(jnp.concatenate([first[r], second[r]], axis=0))
            for h in range(16):
                send[2 * p + half, h, HS * t : HS * t + HS, :] = vt[HS * h : HS * h + HS, :]

    def send_heads(s):
        for k in range(1, 16):
            dev = seq_peer(pos, k)
            remote(send.at[s, dev[0]], recv.at[s, me], q1s.at[s, k], q1r.at[s, k], dev).start()
        recv[s, me] = send[s, me]

    def col(ref, b, start, size):
        return ref.at[b // 3, pl.ds(pl.multiple_of(lax.rem(b, 3) * 1024 + start, 128), size)]

    def half_rows(ib):
        i = lax.rem(me // 8 + 1 + ib, 2)
        return i, pl.multiple_of(i * R, R)

    def qk_part(p):
        ad = adapted[128 * p : 128 * p + 128]
        put_heads(p, 0, dot(ad, wq[...]) * (LOG2E / math.sqrt(HS)), dot(ad, wk[...]))

    qk_part(0)

    for c in bias_in:
        c.wait()
    twin = lax.rem(samp + 4, 8)

    def bias_copy(ib, b, ss, rs, dev, src=None):
        r0 = half_rows(ib)[1]
        dst = col(G, b, r0, R)
        return remote(dst if src is None else src.at[pl.ds(r0, R)], dst, ss, rs, dev)

    def bias_y(ib):
        return bias_copy(ib, samp, bys.at[ib], byr.at[ib], samp_peer(pos, 4), BR)

    def bias_x(ib, k):
        return bias_copy(ib, samp, bxs.at[ib, k], bxr.at[ib, k], along(pos, "x", k), BR)

    def bias_f(ib, k):
        return bias_copy(ib, twin, bfs.at[ib, k], bfr.at[ib, k], along(pos, "x", k))

    for ib in range(2):
        bias_y(ib).start()
    for k in range(1, 4):
        bias_x(0, k).start()
    G[samp // 3, pl.ds(pl.multiple_of(lax.rem(samp, 3) * 1024, 1024), 1024), :] = BR[...]

    def va_part(p):
        r = slice(128 * p, 128 * p + 128)
        gate = jax.nn.sigmoid(dot(adapted[r], wg[...]))
        sig[r, :] = gate
        dg = dot(dp[r], wo[...], 1, 1)
        dgated[r, :] = dg
        put_heads(p, 1, dot(adapted[r], wv[...]), dg * gate)
        send_heads(2 * p)
        send_heads(2 * p + 1)

    va_part(0)

    for ib in range(2):
        if ib == 1:
            for k in range(1, 4):
                bias_x(1, k).start()
        bias_y(ib).wait()
        for k in range(1, 4):
            bias_f(ib, k).start()

    qk_part(1)
    va_part(1)
    adT[...] = jnp.transpose(adapted)

    live = mask[...] > 0
    livef = live.astype(f32)
    db_copies = []
    for ib in range(2):
        i, r0 = half_rows(ib)
        rows = pl.ds(r0, R)
        for k in range(1, 4):
            bias_x(ib, k).wait()
            bias_f(ib, k).wait()

        def prep(n, c):
            part = pl.ds(pl.multiple_of(n * 128, 128), 128)
            for b in range(8):
                sl = slice(128 * b, 128 * b + 128)
                tile = G[b // 3, pl.ds(pl.multiple_of(1024 * (b % 3) + r0 + n * 128, 128), 128), :]
                bm[part, sl] = jnp.where(live[:, sl], tile.astype(f32) * LOG2E, masked_score)
                acc[part, sl] = jnp.zeros((128, 128), f32)
            return c

        lax.fori_loop(0, R // 128, prep, 0)

        def sample(s, carry):
            if ib == 0:
                for k in range(1, 16):
                    remote(send.at[s, 0], recv.at[s, 0], q1s.at[s, k], q1r.at[s, k], seq_peer(pos, k)).wait()
                lo64, hi64 = slice(0, 64), slice(64, 128)
                for t, (r, l) in enumerate(((0, lo64), (0, hi64), (48, lo64), (48, hi64))):
                    for b in range(8):
                        sl = slice(128 * b, 128 * b + 128)
                        both = jnp.concatenate([recv[s, 2 * b, r : r + 48, l], recv[s, 2 * b + 1, r : r + 48, l]], axis=1)
                        if t == 1:
                            both = jnp.where(live[:, sl], both.astype(f32), 0.0).astype(bf16)
                        xs[s, 48 * t : 48 * t + 48, sl] = both
            qT = xs[s, 0:48, rows]
            kT = xs[s, 48:96, :]
            vext = jnp.concatenate([xs[s, 96:144, :], jnp.ones((16, T), bf16)], axis=0)
            S = dot(qT, kT, 0, 0) + bm[...]
            m = jnp.max(S, axis=1, keepdims=True)
            e = jnp.exp2(S - m)
            eb = e.astype(bf16)
            av = dot(vext, eb, 1, 1)
            rinv = 1.0 / av[48:49]
            att = av[0:48] * rinv
            da = (xs[s, 144:192, rows].astype(f32) * rinv).astype(bf16)
            delta = jnp.sum(da.astype(f32) * att, axis=0, keepdims=True)
            hi = delta.astype(bf16).astype(f32)
            row = lax.broadcasted_iota(jnp.int32, (16, R), 0)
            corr = jnp.where(row == 0, -hi, jnp.where(row == 1, hi - delta, 0.0)).astype(bf16)
            dS = e * dot(jnp.concatenate([da, corr], axis=0), vext, 0, 0)
            acc[...] += dS
            dSb = dS.astype(bf16)
            dq = (dot(kT, dSb, 1, 1) * (1.0 / math.sqrt(HS))).astype(bf16)
            dk = dot(qT, dSb)
            dv = dot(da, eb)
            att = att.astype(bf16)

            for r in range(8):
                dev = 8 * i + r
                lanes = slice(64 * r, 64 * r + 64)
                send[s, dev, 0:48, :] = jnp.concatenate([att[:, lanes], dq[:, lanes]], axis=1)
            for r in range(8):
                dev = 8 * i + r

                def go():
                    k = lax.rem(dev - me + 16, 16)
                    remote(send.at[s, dev, 0:48], back.at[s, me, 0:48], o1s.at[s, k], o1r.at[s, k], (dev, samp)).start()

                if ib == 0:
                    go()
                else:
                    pl.when(dev != me)(go)
            if ib == 0:
                dkv[s, 0:48, :] = dk
                dkv[s, 48:96, :] = dv
            else:
                back[s, me, 0:48, :] = send[s, me, 0:48, :]
                dk = ((dkv[s, 0:48, :] + dk) * (livef * LN2)).astype(bf16)
                dv = (dkv[s, 48:96, :] + dv).astype(bf16)
                for n in range(16):
                    lanes = slice(64 * n, 64 * n + 64)
                    send[s, n, 48:96, :] = jnp.concatenate([dk[:, lanes], dv[:, lanes]], axis=1)
                for k in range(1, 16):
                    dev = seq_peer(pos, k)
                    remote(send.at[s, dev[0], 48:96], back.at[s, me, 48:96], o2s.at[s, k], o2r.at[s, k], dev).start()
                back[s, me, 48:96, :] = send[s, me, 48:96, :]
            return carry

        lax.fori_loop(0, 4, sample, 0)

        def fin(n, c):
            part = pl.ds(pl.multiple_of(n * 128, 128), 128)
            for b in range(8):
                sl = slice(128 * b, 128 * b + 128)
                DBS[b, pl.ds(pl.multiple_of(r0 + n * 128, 128), 128), :] = (acc[part, sl] * livef[:, sl]).astype(bf16)
            return c

        lax.fori_loop(0, R // 128, fin, 0)
        for k in range(1, 4):
            dev = along(pos, "x", k)
            for y in range(2):
                c = remote(DBS.at[lax.rem(dev[1], 4) + 4 * y, rows], DB.at[k - 1, y, rows],
                           dbs.at[ib, 2 * k + y], dbr.at[ib, 2 * k + y], dev)
                c.start()
                db_copies.append(c)

    def get(t):
        both = [
            jnp.transpose(jnp.concatenate([back[s, h, HS * t : HS * t + HS, :] for h in range(16)], axis=0))
            for s in range(4)
        ]
        return jnp.concatenate([z[0:64] for z in both], axis=0), jnp.concatenate([z[64:128] for z in both], axis=0)

    first = {}
    place = {4: 0, 3: 1, 0: 2, 1: 3, 2: 4}

    def put(m, val):
        at = place[m]
        rows = slice(768 * at, 768 * at + 768)
        for j in range(6):
            G[j, rows, :] = val[:, 128 * j : 128 * j + 128].astype(bf16)
        first[at] = []
        for p in range(3):
            c = remote(G.at[other * 3 + p, rows], R0.at[p, rows], s0s.at[p, at], s0r.at[p, at], core_peer(pos))
            c.start()
            first[at].append(c)

    groups = [(0, 2304, R1a, B1a, R2a, R3a), (2304, 1536, R1b, B1b, R2b, R3b)]
    flying = {}

    def quarter(g, i):
        base, n = groups[g][:2]
        return pl.ds(pl.multiple_of(base + i * (n // 4), 16), n // 4)

    def piece(g, i):
        n = groups[g][1] // 16
        return pl.ds(pl.multiple_of(i * n, 16), n)

    def ring(key, g, p, axis, ss, rs, ref):
        out = []
        for k in range(1, 4):
            src, dst = ref(k)
            c = remote(src, dst, ss.at[g, p, k], rs.at[g, p, k], along(pos, axis, k))
            c.start()
            out.append(c)
        flying[key, g, p] = out

    def land(key, g, p):
        for c in flying[key, g, p]:
            c.wait()

    def scatter1(g):
        base, n, R1 = groups[g][:3]
        for at in range(base // 768, (base + n) // 768):
            for c in first[at]:
                c.wait()
        for p in range(3):
            j = mine[p]
            a1 = AXES[p][0]

            def add(i, carry):
                rows = pl.ds(pl.multiple_of(base + i * 384, 384), 384)
                G[j, rows, :] = (G[j, rows, :].astype(f32) + R0[p, rows, :].astype(f32)).astype(bf16)
                return carry

            lax.fori_loop(0, n // 384, add, 0)
            ring("s1", g, p, a1, s1s, s1r, lambda k: (G.at[j, quarter(g, lax.rem(pos[a1] + k, 4))], R1.at[p, k - 1]))

    def scatter2(g):
        R1, B1, R2 = groups[g][2:5]
        for p in range(3):
            land("s1", g, p)
            a1, a2 = AXES[p][0], AXES[p][1]
            tot = G[mine[p], quarter(g, pos[a1]), :].astype(f32)
            for k in range(3):
                tot = tot + R1[p, k].astype(f32)
            B1[p] = tot.astype(bf16)
            ring("s2", g, p, a2, s2s, s2r, lambda k: (B1.at[p, piece(g, lax.rem(pos[a2] + k, 4))], R2.at[p, k - 1]))

    def exchange(g):
        B1, R2, R3 = groups[g][3:6]
        for p in range(3):
            land("s2", g, p)
            a2, a3 = AXES[p][1], AXES[p][2]
            tot = B1[p, piece(g, pos[a2]), :].astype(f32)
            for k in range(3):
                tot = tot + R2[p, k].astype(f32)
            at = pos[a3]
            R3[p, at] = tot.astype(bf16)
            ring("s3", g, p, a3, s3s, s3r, lambda k: (R3.at[p, at], R3.at[p, at]))

    def gather2(g):
        base, n = groups[g][:2]
        R3 = groups[g][5]
        for p in range(3):
            land("s3", g, p)
            a1, a2 = AXES[p][0], AXES[p][1]
            rows = pl.ds(pl.multiple_of(base + pos[a1] * (n // 4) + pos[a2] * (n // 16), 16), n // 16)
            F[mine[p], rows, :] = (
                R3[p, 0].astype(f32) + R3[p, 1].astype(f32) + R3[p, 2].astype(f32) + R3[p, 3].astype(f32)
            ).astype(bf16)
            ring("g2", g, p, a2, g2s, g2r, lambda k: (F.at[mine[p], rows], F.at[mine[p], rows]))

    cgc = []

    def to_core(g, p, k, t):
        part = F.at[mine[p], quarter(g, t)]
        c = remote(part, part, gcs.at[g, p, k], gcr.at[g, p, k], core_peer(pos))
        c.start()
        cgc.append(c)

    def gather1(g):
        for p in range(3):
            land("g2", g, p)
            a1 = AXES[p][0]
            part = F.at[mine[p], quarter(g, pos[a1])]
            ring("g1", g, p, a1, g1s, g1r, lambda k: (part, part))
            to_core(g, p, 0, pos[a1])

    def gather0(g):
        for p in range(3):
            for k in range(1, 4):
                flying["g1", g, p][k - 1].wait()
                to_core(g, p, k, lax.rem(pos[AXES[p][0]] + 4 - k, 4))

    def home(r, ss, rs):
        for s in range(4):
            for k in range(1, 16):
                part = slice(r, r + 48)
                remote(send.at[s, 0, part], back.at[s, 0, part], ss.at[s, k], rs.at[s, k], seq_peer(pos, k)).wait()

    home(0, o1s, o1r)
    cot = dout[...].astype(f32)
    gs = sig[...]
    att, dq = get(0)
    att = att.astype(f32)
    gated = (gs * att).astype(bf16)
    put(4, dot(gated, dproj[...], 0, 0))
    dgl = (dgated[...] * att * gs * (1.0 - gs)).astype(bf16)
    put(3, dot(adT[...], dgl))
    put(0, dot(adT[...], dq))
    scatter1(0)
    home(48, o2s, o2r)
    dk, dv = get(1)
    dxs = [dq, dk, dv]
    put(1, dot(adT[...], dk))
    put(2, dot(adT[...], dv))
    scatter1(1)

    normed, inv = norm_rows(tok[...].astype(f32))
    dog[...] = (cot * dot(gated, wo[...])).astype(bf16)
    d_ad = dot(dgl, wg[...], 1, 1)
    for m, w in enumerate((wq, wk, wv)):
        d_ad = d_ad + dot(dxs[m], w[...], 1, 1)
    dshift[...] = d_ad.astype(bf16)
    dscale[...] = (d_ad * normed).astype(bf16)
    dn = d_ad * scale[...].astype(f32)
    m1 = jnp.mean(dn, axis=-1, keepdims=True)
    m2 = jnp.mean(dn * normed, axis=-1, keepdims=True)
    dtok[...] = (cot + inv * (dn - m1 - normed * m2)).astype(bf16)

    scatter2(0)
    scatter2(1)

    for c in db_copies:
        c.wait()

    def sum_bias(i, carry):
        rows = pl.ds(pl.multiple_of(i * 128, 128), 128)
        for y in range(2):
            b = pos["x"] + 4 * y
            tot = DBS[b, rows, :].astype(f32)
            for k in range(3):
                tot = tot + DB[k, y, rows, :].astype(f32)
            SB[y, rows, :] = tot.astype(bf16)
        return carry

    lax.fori_loop(0, 8, sum_bias, 0)
    yhi = samp // 4
    hand = remote(SB.at[1 - yhi], DY, dys.at[0], dyr.at[0], samp_peer(pos, 4))
    hand.start()

    exchange(0)
    exchange(1)
    gather2(0)
    gather2(1)
    gather1(0)
    gather1(1)

    hand.wait()

    def sum_half(i, carry):
        rows = pl.ds(pl.multiple_of(i * 128, 128), 128)
        SB[yhi, rows, :] = (SB[yhi, rows, :].astype(f32) + DY[rows, :].astype(f32)).astype(bf16)
        return carry

    lax.fori_loop(0, 8, sum_half, 0)
    pr = []
    for k in range(1, 16):
        dev = seq_peer(pos, k)
        rows = pl.ds(pl.multiple_of(dev[0] * 64, 64), 64)
        c = remote(SB.at[yhi, rows], RP.at[me], prs.at[k - 1], prr.at[k - 1], dev)
        c.start()
        pr.append(c)
    RP[me] = SB[yhi, pl.ds(pl.multiple_of(me * 64, 64), 64), :]

    gather0(0)
    gather0(1)
    for c in pr + cgc:
        c.wait()


def widen_kernel(F, RP, *refs):
    acts, outs = refs[:4], refs[4:]
    for i in range(4):
        outs[i][...] = acts[i][...]
    outs[4][...] = RP[...].astype(f32)
    for m, at in ((0, 2), (1, 3), (2, 4), (3, 1), (4, 0)):
        for j in range(6):
            outs[5 + m][:, 128 * j : 128 * j + 128] = F[j, at].astype(f32)


def sds(shape, dtype):
    return jax.ShapeDtypeStruct(shape, dtype)


def on_device(tokens, ada_scale, ada_shift, out_gate, d_out, pair_bias, key_mask,
              w_query, w_key, w_value, w_gate, w_output):
    dma = lambda *shape: pltpu.SemaphoreType.DMA(shape)
    rows = lambda a: a.reshape(256, 768)
    tok, scale, shift, og, cot = map(rows, (tokens, ada_scale, ada_shift, out_gate, d_out))
    heads = V((4, 16, 96, 128), bf16)
    dtok, dscale, dshift, dog, F, RP = pl.pallas_call(
        block_kernel,
        out_shape=(sds((256, 768), bf16),) * 4 + (sds((6, 3840, 128), bf16), sds((16, 64, 128), bf16)),
        in_specs=[spec()] * 12,
        out_specs=[spec()] * 6,
        scratch_shapes=[heads, heads, heads, V((1024, 128), bf16), V((512, 1024), f32), V((512, 1024), f32),
                        V((4, 192, 1024), bf16), V((4, 96, 1024), f32), V((256, 768), f32), V((256, 768), f32), V((768, 256), bf16), V((256, 768), bf16),
                        V((6, 3840, 128), bf16), V((3, 3840, 128), bf16)]
        + [V(shape, bf16) for q in (576, 384)
           for shape in ((3, 3, q, 128), (3, q, 128), (3, 3, q // 4, 128), (3, 4, q // 4, 128))]
        + [V((8, 1024, 128), bf16), V((3, 2, 1024, 128), bf16), V((2, 1024, 128), bf16), V((1024, 128), bf16)]
        + [dma(16)] * 2 + [dma(4, 4)] * 2 + [dma(4)] * 2 + [dma(4, 4)] * 2 + [dma(4, 16)] * 6
        + [dma(3, 5)] * 2 + [dma(2, 3, 4)] * 12 + [dma(2, 8)] * 2 + [dma(1)] * 2 + [dma(15)] * 2,
        compiler_params=pltpu.CompilerParams(vmem_limit_bytes=VMEM_LIMIT, collective_id=2, has_side_effects=True),
        cost_estimate=pl.CostEstimate(flops=16 * 10**9, bytes_accessed=20 << 20, transcendentals=5 << 20),
    )(tok, scale, shift, og, cot, pair_bias, key_mask.reshape(1, 1024), w_query, w_key, w_value, w_gate, w_output)
    act = pl.BlockSpec((32, 768), lambda i: (i, 0))
    tile = pl.BlockSpec((2, 64, 128), lambda i: (i, 0, 0))
    outs = pl.pallas_call(
        widen_kernel,
        grid=(8,),
        out_shape=(sds((256, 768), bf16),) * 4 + (sds((16, 64, 128), f32),) + (sds((768, 768), f32),) * 5,
        in_specs=[pl.BlockSpec((6, 5, 96, 128), lambda i: (0, 0, i, 0)), tile] + [act] * 4,
        out_specs=[act] * 4 + [tile] + [pl.BlockSpec((96, 768), lambda i: (i, 0))] * 5,
    )(F.reshape(6, 5, 768, 128), RP, dtok, dscale, dshift, dog)
    shaped = lambda a: a.reshape(4, 64, 768)
    return tuple(map(shaped, outs[:4])) + tuple(outs[4:])


def solution(mesh):
    act = P("samp", "seq", None)
    tile = P(None, "seq", "samp")
    return jax.shard_map(
        on_device,
        mesh=mesh,
        in_specs=(act,) * 5 + (tile,) + (P(),) * 6,
        out_specs=(act,) * 4 + (tile,) + (P(),) * 5,
        check_vma=False,
    )
```

```python
import functools
import math

import jax
import jax.numpy as jnp
from jax import lax
from jax.experimental import pallas as pl
from jax.experimental.pallas import tpu as pltpu
from jax.sharding import PartitionSpec as P

norm_eps = 1e-05
masked_score = -1e9
HS = 48
LOG2E = 1.4426950408889634
LN2 = 0.6931471805599453
f32 = jnp.float32
bf16 = jnp.bfloat16
V = pltpu.VMEM
VMEM_LIMIT = 62 << 20


def spec():
    return pl.BlockSpec(memory_space=V)


def dot(a, b, ca=1, cb=0):
    return lax.dot_general(a, b, (((ca,), (cb,)), ((), ())), preferred_element_type=f32)


def norm_rows(x):
    mean = jnp.mean(x, axis=-1, keepdims=True)
    centred = x - mean
    var = jnp.mean(centred * centred, axis=-1, keepdims=True)
    inv = lax.rsqrt(var + norm_eps)
    return centred * inv, inv


def position():
    seq, samp = lax.axis_index("seq"), lax.axis_index("samp")
    return {
        "seq": seq,
        "samp": samp,
        "core": lax.rem(seq, 2),
        "z": lax.rem(seq // 2, 4),
        "x": lax.rem(samp, 4),
        "y": (samp // 4) * 2 + seq // 8,
    }


def along(pos, axis, step):
    new = dict(pos)
    new[axis] = lax.rem(pos[axis] + step, 4)
    return ((lax.rem(new["y"], 2)) * 8 + new["z"] * 2 + pos["core"], (new["y"] // 2) * 4 + new["x"])


def seq_peer(pos, step):
    return (lax.rem(pos["seq"] + step, 16), pos["samp"])


def samp_peer(pos, step):
    return (pos["seq"], lax.rem(pos["samp"] + step, 8))


def core_peer(pos):
    return (pos["seq"] + 1 - 2 * pos["core"], pos["samp"])


def remote(src, dst, ss, rs, dev):
    return pltpu.make_async_remote_copy(
        src_ref=src, dst_ref=dst, send_sem=ss, recv_sem=rs, device_id=dev, device_id_type=pl.DeviceIdType.MESH
    )


def greet(devices):
    barrier = pltpu.get_barrier_semaphore()
    for d in devices:
        pl.semaphore_signal(barrier, inc=1, device_id=d, device_id_type=pl.DeviceIdType.MESH)
    return lambda: pl.semaphore_wait(barrier, len(devices))


AXES = (("x", "y", "z"), ("y", "z", "x"), ("z", "x", "y"))


def block_kernel(tok, scale, shift, og, dout, pbias, mask, wq_in, wk_in, wv_in, wg_in, wo_in,
                 dtok, dscale, dshift, dog, F_out, RP, F, W,
                 send, recv, back, BR, bm, acc, xs, dkv, sig, dgated, adT, dproj,
                 G, R0, R1a, B1a, R2a, R3a, R1b, B1b, R2b, R3b, DBS, DB, SB, DY,
                 bas, bar, bxs, bxr, bys, byr, bfs, bfr, q1s, q1r, o1s, o1r, o2s, o2r,
                 s0s, s0r, s1s, s1r, s2s, s2r, s3s, s3r, g2s, g2r, g1s, g1r, gcs, gcr, dbs, dbr, dys, dyr, prs, prr, ws, fs):
    T = 1024
    R = 512
    wq, wk, wv, wg, wo = (W.at[n] for n in range(5))
    loads = [pltpu.make_async_copy(w, W.at[n], ws.at[n]) for n, w in enumerate((wq_in, wk_in, wv_in, wg_in, wo_in))]
    for c in loads:
        c.start()
    pos = position()
    me = pos["seq"]
    samp = pos["samp"]
    core = pos["core"]
    other = 1 - core
    mine = [core * 3 + p for p in range(3)]
    peers = [seq_peer(pos, k) for k in range(1, 16)] + [samp_peer(pos, k) for k in range(1, 8)]
    far_y = along(pos, "y", jnp.where(lax.rem(pos["y"], 2) == 0, 3, 1))
    arrived = greet(peers + [far_y])

    normed, inv = norm_rows(tok[...].astype(f32))
    adapted = (normed * scale[...].astype(f32) + shift[...].astype(f32)).astype(bf16)
    dp = (dout[...].astype(f32) * og[...].astype(f32)).astype(bf16)
    dproj[...] = dp

    for c in loads:
        c.wait()
    arrived()
    bias_in = []
    for k in range(1, 16):
        dev = seq_peer(pos, k)
        c = remote(pbias.at[dev[0]], BR.at[pl.ds(pl.multiple_of(me * 64, 64), 64)], bas.at[k], bar.at[k], dev)
        c.start()
        bias_in.append(c)
    BR[pl.ds(pl.multiple_of(me * 64, 64), 64), :] = pbias[me]

    def put_heads(p, t, first, second):
        first, second = first.astype(bf16), second.astype(bf16)
        for half in range(2):
            r = slice(64 * half, 64 * half + 64)
            vt = jnp.transpose(jnp.concatenate([first[r], second[r]], axis=0))
            for h in range(16):
                send[2 * p + half, h, HS * t : HS * t + HS, :] = vt[HS * h : HS * h + HS, :]

    def send_heads(s):
        for k in range(1, 16):
            dev = seq_peer(pos, k)
            remote(send.at[s, dev[0]], recv.at[s, me], q1s.at[s, k], q1r.at[s, k], dev).start()
        recv[s, me] = send[s, me]

    def col(ref, b, start, size):
        return ref.at[b // 3, pl.ds(pl.multiple_of(lax.rem(b, 3) * 1024 + start, 128), size)]

    def half_rows(ib):
        i = lax.rem(me // 8 + 1 + ib, 2)
        return i, pl.multiple_of(i * R, R)

    def qk_part(p):
        ad = adapted[128 * p : 128 * p + 128]
        put_heads(p, 0, dot(ad, wq[...]) * (LOG2E / math.sqrt(HS)), dot(ad, wk[...]))

    qk_part(0)

    for c in bias_in:
        c.wait()
    twin = lax.rem(samp + 4, 8)

    def bias_copy(ib, b, ss, rs, dev, src=None):
        r0 = half_rows(ib)[1]
        dst = col(G, b, r0, R)
        return remote(dst if src is None else src.at[pl.ds(r0, R)], dst, ss, rs, dev)

    def bias_y(ib):
        return bias_copy(ib, samp, bys.at[ib], byr.at[ib], samp_peer(pos, 4), BR)

    def bias_x(ib, k):
        return bias_copy(ib, samp, bxs.at[ib, k], bxr.at[ib, k], along(pos, "x", k), BR)

    def bias_f(ib, k):
        return bias_copy(ib, twin, bfs.at[ib, k], bfr.at[ib, k], along(pos, "x", k))

    for ib in range(2):
        bias_y(ib).start()
    for k in range(1, 4):
        bias_x(0, k).start()
    G[samp // 3, pl.ds(pl.multiple_of(lax.rem(samp, 3) * 1024, 1024), 1024), :] = BR[...]

    def va_part(p):
        r = slice(128 * p, 128 * p + 128)
        gate = jax.nn.sigmoid(dot(adapted[r], wg[...]))
        sig[r, :] = gate
        dg = dot(dp[r], wo[...], 1, 1)
        dgated[r, :] = dg
        put_heads(p, 1, dot(adapted[r], wv[...]), dg * gate)
        send_heads(2 * p)
        send_heads(2 * p + 1)

    va_part(0)

    for ib in range(2):
        if ib == 1:
            for k in range(1, 4):
                bias_x(1, k).start()
        bias_y(ib).wait()
        for k in range(1, 4):
            bias_f(ib, k).start()

    qk_part(1)
    va_part(1)
    adT[...] = jnp.transpose(adapted)

    live = mask[...] > 0
    livef = live.astype(f32)
    db_copies = []
    for ib in range(2):
        i, r0 = half_rows(ib)
        rows = pl.ds(r0, R)
        for k in range(1, 4):
            bias_x(ib, k).wait()
            bias_f(ib, k).wait()

        def prep(n, c):
            part = pl.ds(pl.multiple_of(n * 128, 128), 128)
            for b in range(8):
                sl = slice(128 * b, 128 * b + 128)
                tile = G[b // 3, pl.ds(pl.multiple_of(1024 * (b % 3) + r0 + n * 128, 128), 128), :]
                bm[part, sl] = jnp.where(live[:, sl], tile.astype(f32) * LOG2E, masked_score)
                acc[part, sl] = jnp.zeros((128, 128), f32)
            return c

        lax.fori_loop(0, R // 128, prep, 0)

        def sample(s, carry):
            if ib == 0:
                for k in range(1, 16):
                    remote(send.at[s, 0], recv.at[s, 0], q1s.at[s, k], q1r.at[s, k], seq_peer(pos, k)).wait()
                lo64, hi64 = slice(0, 64), slice(64, 128)
                for t, (r, l) in enumerate(((0, lo64), (0, hi64), (48, lo64), (48, hi64))):
                    for b in range(8):
                        sl = slice(128 * b, 128 * b + 128)
                        both = jnp.concatenate([recv[s, 2 * b, r : r + 48, l], recv[s, 2 * b + 1, r : r + 48, l]], axis=1)
                        if t == 1:
                            both = jnp.where(live[:, sl], both.astype(f32), 0.0).astype(bf16)
                        xs[s, 48 * t : 48 * t + 48, sl] = both
            qT = xs[s, 0:48, rows]
            kT = xs[s, 48:96, :]
            vext = jnp.concatenate([xs[s, 96:144, :], jnp.ones((16, T), bf16)], axis=0)
            S = dot(qT, kT, 0, 0) + bm[...]
            m = jnp.max(S, axis=1, keepdims=True)
            e = jnp.exp2(S - m)
            eb = e.astype(bf16)
            av = dot(vext, eb, 1, 1)
            rinv = 1.0 / av[48:49]
            att = av[0:48] * rinv
            da = (xs[s, 144:192, rows].astype(f32) * rinv).astype(bf16)
            delta = jnp.sum(da.astype(f32) * att, axis=0, keepdims=True)
            hi = delta.astype(bf16).astype(f32)
            row = lax.broadcasted_iota(jnp.int32, (16, R), 0)
            corr = jnp.where(row == 0, -hi, jnp.where(row == 1, hi - delta, 0.0)).astype(bf16)
            dS = e * dot(jnp.concatenate([da, corr], axis=0), vext, 0, 0)
            acc[...] += dS
            dSb = dS.astype(bf16)
            dq = (dot(kT, dSb, 1, 1) * (1.0 / math.sqrt(HS))).astype(bf16)
            dk = dot(qT, dSb)
            dv = dot(da, eb)
            att = att.astype(bf16)

            for r in range(8):
                dev = 8 * i + r
                lanes = slice(64 * r, 64 * r + 64)
                send[s, dev, 0:48, :] = jnp.concatenate([att[:, lanes], dq[:, lanes]], axis=1)
            for r in range(8):
                dev = 8 * i + r

                def go():
                    k = lax.rem(dev - me + 16, 16)
                    remote(send.at[s, dev, 0:48], back.at[s, me, 0:48], o1s.at[s, k], o1r.at[s, k], (dev, samp)).start()

                if ib == 0:
                    go()
                else:
                    pl.when(dev != me)(go)
            if ib == 0:
                dkv[s, 0:48, :] = dk
                dkv[s, 48:96, :] = dv
            else:
                back[s, me, 0:48, :] = send[s, me, 0:48, :]
                dk = ((dkv[s, 0:48, :] + dk) * (livef * LN2)).astype(bf16)
                dv = (dkv[s, 48:96, :] + dv).astype(bf16)
                for n in range(16):
                    lanes = slice(64 * n, 64 * n + 64)
                    send[s, n, 48:96, :] = jnp.concatenate([dk[:, lanes], dv[:, lanes]], axis=1)
                for k in range(1, 16):
                    dev = seq_peer(pos, k)
                    remote(send.at[s, dev[0], 48:96], back.at[s, me, 48:96], o2s.at[s, k], o2r.at[s, k], dev).start()
                back[s, me, 48:96, :] = send[s, me, 48:96, :]
            return carry

        lax.fori_loop(0, 4, sample, 0)

        def fin(n, c):
            part = pl.ds(pl.multiple_of(n * 128, 128), 128)
            for b in range(8):
                sl = slice(128 * b, 128 * b + 128)
                DBS[b, pl.ds(pl.multiple_of(r0 + n * 128, 128), 128), :] = (acc[part, sl] * livef[:, sl]).astype(bf16)
            return c

        lax.fori_loop(0, R // 128, fin, 0)
        for k in range(1, 4):
            dev = along(pos, "x", k)
            for y in range(2):
                c = remote(DBS.at[lax.rem(dev[1], 4) + 4 * y, rows], DB.at[k - 1, y, rows],
                           dbs.at[ib, 2 * k + y], dbr.at[ib, 2 * k + y], dev)
                c.start()
                db_copies.append(c)

    def get(t):
        both = [
            jnp.transpose(jnp.concatenate([back[s, h, HS * t : HS * t + HS, :] for h in range(16)], axis=0))
            for s in range(4)
        ]
        return jnp.concatenate([z[0:64] for z in both], axis=0), jnp.concatenate([z[64:128] for z in both], axis=0)

    first = {}
    place = {4: 0, 3: 1, 0: 2, 1: 3, 2: 4}

    def put(m, val):
        at = place[m]
        rows = slice(768 * at, 768 * at + 768)
        for j in range(6):
            G[j, rows, :] = val[:, 128 * j : 128 * j + 128].astype(bf16)
        first[at] = []
        for p in range(3):
            c = remote(G.at[other * 3 + p, rows], R0.at[p, rows], s0s.at[p, at], s0r.at[p, at], core_peer(pos))
            c.start()
            first[at].append(c)

    groups = [(0, 2304, R1a, B1a, R2a, R3a), (2304, 1536, R1b, B1b, R2b, R3b)]
    flying = {}

    def quarter(g, i):
        base, n = groups[g][:2]
        return pl.ds(pl.multiple_of(base + i * (n // 4), 16), n // 4)

    def piece(g, i):
        n = groups[g][1] // 16
        return pl.ds(pl.multiple_of(i * n, 16), n)

    def ring(key, g, p, axis, ss, rs, ref):
        out = []
        for k in range(1, 4):
            src, dst = ref(k)
            c = remote(src, dst, ss.at[g, p, k], rs.at[g, p, k], along(pos, axis, k))
            c.start()
            out.append(c)
        flying[key, g, p] = out

    def land(key, g, p):
        for c in flying[key, g, p]:
            c.wait()

    def scatter1(g):
        base, n, R1 = groups[g][:3]
        for at in range(base // 768, (base + n) // 768):
            for c in first[at]:
                c.wait()
        for p in range(3):
            j = mine[p]
            a1 = AXES[p][0]

            def add(i, carry):
                rows = pl.ds(pl.multiple_of(base + i * 384, 384), 384)
                G[j, rows, :] = (G[j, rows, :].astype(f32) + R0[p, rows, :].astype(f32)).astype(bf16)
                return carry

            lax.fori_loop(0, n // 384, add, 0)
            ring("s1", g, p, a1, s1s, s1r, lambda k: (G.at[j, quarter(g, lax.rem(pos[a1] + k, 4))], R1.at[p, k - 1]))

    def scatter2(g):
        R1, B1, R2 = groups[g][2:5]
        for p in range(3):
            land("s1", g, p)
            a1, a2 = AXES[p][0], AXES[p][1]
            tot = G[mine[p], quarter(g, pos[a1]), :].astype(f32)
            for k in range(3):
                tot = tot + R1[p, k].astype(f32)
            B1[p] = tot.astype(bf16)
            ring("s2", g, p, a2, s2s, s2r, lambda k: (B1.at[p, piece(g, lax.rem(pos[a2] + k, 4))], R2.at[p, k - 1]))

    def exchange(g):
        B1, R2, R3 = groups[g][3:6]
        for p in range(3):
            land("s2", g, p)
            a2, a3 = AXES[p][1], AXES[p][2]
            tot = B1[p, piece(g, pos[a2]), :].astype(f32)
            for k in range(3):
                tot = tot + R2[p, k].astype(f32)
            at = pos[a3]
            R3[p, at] = tot.astype(bf16)
            ring("s3", g, p, a3, s3s, s3r, lambda k: (R3.at[p, at], R3.at[p, at]))

    def gather2(g):
        base, n = groups[g][:2]
        R3 = groups[g][5]
        for p in range(3):
            land("s3", g, p)
            a1, a2 = AXES[p][0], AXES[p][1]
            rows = pl.ds(pl.multiple_of(base + pos[a1] * (n // 4) + pos[a2] * (n // 16), 16), n // 16)
            F[mine[p], rows, :] = (
                R3[p, 0].astype(f32) + R3[p, 1].astype(f32) + R3[p, 2].astype(f32) + R3[p, 3].astype(f32)
            ).astype(bf16)
            ring("g2", g, p, a2, g2s, g2r, lambda k: (F.at[mine[p], rows], F.at[mine[p], rows]))

    cgc = [[], []]

    def to_core(g, p, k, t):
        part = F.at[mine[p], quarter(g, t)]
        c = remote(part, part, gcs.at[g, p, k], gcr.at[g, p, k], core_peer(pos))
        c.start()
        cgc[g].append(c)

    def quarter_part(g, i, half):
        base, n = groups[g][:2]
        return pl.ds(pl.multiple_of(base + i * (n // 4) + half * (n // 8), 16), n // 8)

    def gather1(g):
        for p in range(3):
            land("g2", g, p)
            a1 = AXES[p][0]
            part = F.at[mine[p], quarter(g, pos[a1])]
            out = []
            for n, k in enumerate((1, 3)):
                c = remote(part, part, g1s.at[g, p, n], g1r.at[g, p, n], along(pos, a1, k))
                c.start()
                out.append(c)
            flying["g1", g, p] = out
            to_core(g, p, 0, pos[a1])

    def forward(g):
        for p in range(3):
            a1 = AXES[p][0]
            out = []
            for n, k in enumerate((1, 3)):
                flying["g1", g, p][n].wait()
                t = lax.rem(pos[a1] + 4 - k, 4)
                part = F.at[mine[p], quarter_part(g, t, n)]
                c = remote(part, part, g1s.at[g, p, 2 + n], g1r.at[g, p, 2 + n], along(pos, a1, k))
                c.start()
                out.append(c)
                to_core(g, p, 1 + n, t)
            flying["f1", g, p] = out

    def gather0(g):
        for p in range(3):
            land("f1", g, p)
            to_core(g, p, 3, lax.rem(pos[AXES[p][0]] + 2, 4))

    def home(r, ss, rs):
        for s in range(4):
            for k in range(1, 16):
                part = slice(r, r + 48)
                remote(send.at[s, 0, part], back.at[s, 0, part], ss.at[s, k], rs.at[s, k], seq_peer(pos, k)).wait()

    home(0, o1s, o1r)
    cot = dout[...].astype(f32)
    gs = sig[...]
    att, dq = get(0)
    att = att.astype(f32)
    gated = (gs * att).astype(bf16)
    put(4, dot(gated, dproj[...], 0, 0))
    dgl = (dgated[...] * att * gs * (1.0 - gs)).astype(bf16)
    put(3, dot(adT[...], dgl))
    put(0, dot(adT[...], dq))
    scatter1(0)
    home(48, o2s, o2r)
    dk, dv = get(1)
    dxs = [dq, dk, dv]
    put(1, dot(adT[...], dk))
    put(2, dot(adT[...], dv))
    scatter1(1)

    normed, inv = norm_rows(tok[...].astype(f32))
    dog[...] = (cot * dot(gated, wo[...])).astype(bf16)
    d_ad = dot(dgl, wg[...], 1, 1)
    for m, w in enumerate((wq, wk, wv)):
        d_ad = d_ad + dot(dxs[m], w[...], 1, 1)
    dshift[...] = d_ad.astype(bf16)
    dscale[...] = (d_ad * normed).astype(bf16)
    dn = d_ad * scale[...].astype(f32)
    m1 = jnp.mean(dn, axis=-1, keepdims=True)
    m2 = jnp.mean(dn * normed, axis=-1, keepdims=True)
    dtok[...] = (cot + inv * (dn - m1 - normed * m2)).astype(bf16)

    scatter2(0)
    scatter2(1)

    for c in db_copies:
        c.wait()

    def sum_bias(i, carry):
        rows = pl.ds(pl.multiple_of(i * 128, 128), 128)
        for y in range(2):
            b = pos["x"] + 4 * y
            tot = DBS[b, rows, :].astype(f32)
            for k in range(3):
                tot = tot + DB[k, y, rows, :].astype(f32)
            SB[y, rows, :] = tot.astype(bf16)
        return carry

    lax.fori_loop(0, 8, sum_bias, 0)
    yhi = samp // 4
    hand = remote(SB.at[1 - yhi], DY, dys.at[0], dyr.at[0], samp_peer(pos, 4))
    hand.start()

    exchange(0)
    exchange(1)
    gather2(0)
    gather2(1)
    gather1(0)
    gather1(1)

    hand.wait()

    def sum_half(i, carry):
        rows = pl.ds(pl.multiple_of(i * 128, 128), 128)
        SB[yhi, rows, :] = (SB[yhi, rows, :].astype(f32) + DY[rows, :].astype(f32)).astype(bf16)
        return carry

    lax.fori_loop(0, 8, sum_half, 0)
    pr = []
    for k in range(1, 16):
        dev = seq_peer(pos, k)
        rows = pl.ds(pl.multiple_of(dev[0] * 64, 64), 64)
        c = remote(SB.at[yhi, rows], RP.at[me], prs.at[k - 1], prr.at[k - 1], dev)
        c.start()
        pr.append(c)
    RP[me] = SB[yhi, pl.ds(pl.multiple_of(me * 64, 64), 64), :]

    forward(0)
    forward(1)
    out_copies = []

    def leave(g, first_slab):
        base, n = groups[g][:2]
        for p in range(3):
            part = (first_slab + p, slice(base, base + n))
            c = pltpu.make_async_copy(F.at[part], F_out.at[part], fs.at[len(out_copies)])
            c.start()
            out_copies.append(c)

    gather0(0)
    leave(0, core * 3)
    gather0(1)
    leave(1, core * 3)
    for g in range(2):
        for c in cgc[g]:
            c.wait()
        leave(g, other * 3)
    for c in pr + out_copies:
        c.wait()


def widen_kernel(F, RP, *refs):
    acts, outs = refs[:4], refs[4:]
    for i in range(4):
        outs[i][...] = acts[i][...]
    outs[4][...] = RP[...].astype(f32)
    for m, at in ((0, 2), (1, 3), (2, 4), (3, 1), (4, 0)):
        for j in range(6):
            outs[5 + m][:, 128 * j : 128 * j + 128] = F[j, at].astype(f32)


def sds(shape, dtype):
    return jax.ShapeDtypeStruct(shape, dtype)


def on_device(tokens, ada_scale, ada_shift, out_gate, d_out, pair_bias, key_mask,
              w_query, w_key, w_value, w_gate, w_output):
    dma = lambda *shape: pltpu.SemaphoreType.DMA(shape)
    rows = lambda a: a.reshape(256, 768)
    tok, scale, shift, og, cot = map(rows, (tokens, ada_scale, ada_shift, out_gate, d_out))
    heads = V((4, 16, 96, 128), bf16)
    dtok, dscale, dshift, dog, F, RP = pl.pallas_call(
        block_kernel,
        out_shape=(sds((256, 768), bf16),) * 4 + (sds((6, 3840, 128), bf16), sds((16, 64, 128), bf16)),
        in_specs=[spec()] * 7 + [pl.BlockSpec(memory_space=pl.ANY)] * 5,
        out_specs=[spec()] * 4 + [pl.BlockSpec(memory_space=pl.ANY), spec()],
        scratch_shapes=[V((6, 3840, 128), bf16), V((5, 768, 768), bf16), heads, heads, heads, V((1024, 128), bf16), V((512, 1024), f32), V((512, 1024), f32),
                        V((4, 192, 1024), bf16), V((4, 96, 1024), f32), V((256, 768), f32), V((256, 768), f32), V((768, 256), bf16), V((256, 768), bf16),
                        V((6, 3840, 128), bf16), V((3, 3840, 128), bf16)]
        + [V(shape, bf16) for q in (576, 384)
           for shape in ((3, 3, q, 128), (3, q, 128), (3, 3, q // 4, 128), (3, 4, q // 4, 128))]
        + [V((8, 1024, 128), bf16), V((3, 2, 1024, 128), bf16), V((2, 1024, 128), bf16), V((1024, 128), bf16)]
        + [dma(16)] * 2 + [dma(4, 4)] * 2 + [dma(4)] * 2 + [dma(4, 4)] * 2 + [dma(4, 16)] * 6
        + [dma(3, 5)] * 2 + [dma(2, 3, 4)] * 12 + [dma(2, 8)] * 2 + [dma(1)] * 2 + [dma(15)] * 2 + [dma(5), dma(12)],
        compiler_params=pltpu.CompilerParams(vmem_limit_bytes=VMEM_LIMIT, collective_id=2, has_side_effects=True),
        cost_estimate=pl.CostEstimate(flops=16 * 10**9, bytes_accessed=20 << 20, transcendentals=5 << 20),
    )(tok, scale, shift, og, cot, pair_bias, key_mask.reshape(1, 1024), w_query, w_key, w_value, w_gate, w_output)
    act = pl.BlockSpec((32, 768), lambda i: (i, 0))
    tile = pl.BlockSpec((2, 64, 128), lambda i: (i, 0, 0))
    outs = pl.pallas_call(
        widen_kernel,
        grid=(8,),
        out_shape=(sds((256, 768), bf16),) * 4 + (sds((16, 64, 128), f32),) + (sds((768, 768), f32),) * 5,
        in_specs=[pl.BlockSpec((6, 5, 96, 128), lambda i: (0, 0, i, 0)), tile] + [act] * 4,
        out_specs=[act] * 4 + [tile] + [pl.BlockSpec((96, 768), lambda i: (i, 0))] * 5,
    )(F.reshape(6, 5, 768, 128), RP, dtok, dscale, dshift, dog)
    shaped = lambda a: a.reshape(4, 64, 768)
    return tuple(map(shaped, outs[:4])) + tuple(outs[4:])


def solution(mesh):
    act = P("samp", "seq", None)
    tile = P(None, "seq", "samp")
    return jax.shard_map(
        on_device,
        mesh=mesh,
        in_specs=(act,) * 5 + (tile,) + (P(),) * 6,
        out_specs=(act,) * 4 + (tile,) + (P(),) * 5,
        check_vma=False,
    )
```

```python
import functools
import math

import jax
import jax.numpy as jnp
from jax import lax
from jax.experimental import pallas as pl
from jax.experimental.pallas import tpu as pltpu
from jax.sharding import PartitionSpec as P

norm_eps = 1e-05
masked_score = -1e9
HS = 48
LOG2E = 1.4426950408889634
LN2 = 0.6931471805599453
f32 = jnp.float32
bf16 = jnp.bfloat16
V = pltpu.VMEM
VMEM_LIMIT = 62 << 20


def spec():
    return pl.BlockSpec(memory_space=V)


def dot(a, b, ca=1, cb=0):
    return lax.dot_general(a, b, (((ca,), (cb,)), ((), ())), preferred_element_type=f32)


def norm_rows(x):
    mean = jnp.mean(x, axis=-1, keepdims=True)
    centred = x - mean
    var = jnp.mean(centred * centred, axis=-1, keepdims=True)
    inv = lax.rsqrt(var + norm_eps)
    return centred * inv, inv


def position():
    seq, samp = lax.axis_index("seq"), lax.axis_index("samp")
    return {
        "seq": seq,
        "samp": samp,
        "core": lax.rem(seq, 2),
        "z": lax.rem(seq // 2, 4),
        "x": lax.rem(samp, 4),
        "y": (samp // 4) * 2 + seq // 8,
    }


def along(pos, axis, step):
    new = dict(pos)
    new[axis] = lax.rem(pos[axis] + step, 4)
    return ((lax.rem(new["y"], 2)) * 8 + new["z"] * 2 + pos["core"], (new["y"] // 2) * 4 + new["x"])


def seq_peer(pos, step):
    return (lax.rem(pos["seq"] + step, 16), pos["samp"])


def samp_peer(pos, step):
    return (pos["seq"], lax.rem(pos["samp"] + step, 8))


def core_peer(pos):
    return (pos["seq"] + 1 - 2 * pos["core"], pos["samp"])


def remote(src, dst, ss, rs, dev):
    return pltpu.make_async_remote_copy(
        src_ref=src, dst_ref=dst, send_sem=ss, recv_sem=rs, device_id=dev, device_id_type=pl.DeviceIdType.MESH
    )


def greet(devices):
    barrier = pltpu.get_barrier_semaphore()
    for d in devices:
        pl.semaphore_signal(barrier, inc=1, device_id=d, device_id_type=pl.DeviceIdType.MESH)
    return lambda: pl.semaphore_wait(barrier, len(devices))


AXES = (("x", "y", "z"), ("y", "z", "x"), ("z", "x", "y"))


def block_kernel(tok, scale, shift, og, dout, pbias, mask, wq_in, wk_in, wv_in, wg_in, wo_in,
                 dtok, dscale, dshift, dog, F_out, RP, F, W,
                 send, recv, back, BR, bm, acc, xs, dkv, sig, dgated, adT, dproj,
                 G, R0, R1a, B1a, R2a, R3a, R1b, B1b, R2b, R3b, DBS, DB, SB, DY,
                 bas, bar, bxs, bxr, bys, byr, bfs, bfr, q1s, q1r, o1s, o1r, o2s, o2r,
                 s0s, s0r, s1s, s1r, s2s, s2r, s3s, s3r, g2s, g2r, g1s, g1r, gcs, gcr, dbs, dbr, dys, dyr, prs, prr, ws, fs):
    T = 1024
    R = 512
    wq, wk, wv, wg, wo = (W.at[n] for n in range(5))
    loads = [pltpu.make_async_copy(w, W.at[n], ws.at[n]) for n, w in enumerate((wq_in, wk_in, wv_in, wg_in, wo_in))]
    for c in loads:
        c.start()
    pos = position()
    me = pos["seq"]
    samp = pos["samp"]
    core = pos["core"]
    other = 1 - core
    mine = [core * 3 + p for p in range(3)]
    peers = [seq_peer(pos, k) for k in range(1, 16)] + [samp_peer(pos, k) for k in range(1, 8)]
    far_y = along(pos, "y", jnp.where(lax.rem(pos["y"], 2) == 0, 3, 1))
    arrived = greet(peers + [far_y])

    normed, inv = norm_rows(tok[...].astype(f32))
    adapted = (normed * scale[...].astype(f32) + shift[...].astype(f32)).astype(bf16)
    dp = (dout[...].astype(f32) * og[...].astype(f32)).astype(bf16)
    dproj[...] = dp

    arrived()
    bias_in = []
    for k in range(1, 16):
        dev = seq_peer(pos, k)
        c = remote(pbias.at[dev[0]], BR.at[pl.ds(pl.multiple_of(me * 64, 64), 64)], bas.at[k], bar.at[k], dev)
        c.start()
        bias_in.append(c)
    BR[pl.ds(pl.multiple_of(me * 64, 64), 64), :] = pbias[me]

    def put_heads(p, t, first, second):
        first, second = first.astype(bf16), second.astype(bf16)
        for half in range(2):
            r = slice(64 * half, 64 * half + 64)
            vt = jnp.transpose(jnp.concatenate([first[r], second[r]], axis=0))
            for h in range(16):
                send[2 * p + half, h, HS * t : HS * t + HS, :] = vt[HS * h : HS * h + HS, :]

    def send_heads(s):
        for k in range(1, 16):
            dev = seq_peer(pos, k)
            remote(send.at[s, dev[0]], recv.at[s, me], q1s.at[s, k], q1r.at[s, k], dev).start()
        recv[s, me] = send[s, me]

    def col(ref, b, start, size):
        return ref.at[b // 3, pl.ds(pl.multiple_of(lax.rem(b, 3) * 1024 + start, 128), size)]

    def half_rows(ib):
        i = lax.rem(me // 8 + 1 + ib, 2)
        return i, pl.multiple_of(i * R, R)

    def qk_part(p):
        ad = adapted[128 * p : 128 * p + 128]
        put_heads(p, 0, dot(ad, wq[...]) * (LOG2E / math.sqrt(HS)), dot(ad, wk[...]))

    for c in loads[:2]:
        c.wait()
    qk_part(0)

    for c in bias_in:
        c.wait()
    twin = lax.rem(samp + 4, 8)

    def bias_copy(ib, b, ss, rs, dev, src=None):
        r0 = half_rows(ib)[1]
        dst = col(G, b, r0, R)
        return remote(dst if src is None else src.at[pl.ds(r0, R)], dst, ss, rs, dev)

    def bias_y(ib):
        return bias_copy(ib, samp, bys.at[ib], byr.at[ib], samp_peer(pos, 4), BR)

    def bias_x(ib, k):
        return bias_copy(ib, samp, bxs.at[ib, k], bxr.at[ib, k], along(pos, "x", k), BR)

    def bias_f(ib, k):
        return bias_copy(ib, twin, bfs.at[ib, k], bfr.at[ib, k], along(pos, "x", k))

    for ib in range(2):
        bias_y(ib).start()
    for k in range(1, 4):
        bias_x(0, k).start()
    G[samp // 3, pl.ds(pl.multiple_of(lax.rem(samp, 3) * 1024, 1024), 1024), :] = BR[...]

    def va_part(p):
        r = slice(128 * p, 128 * p + 128)
        gate = jax.nn.sigmoid(dot(adapted[r], wg[...]))
        sig[r, :] = gate
        dg = dot(dp[r], wo[...], 1, 1)
        dgated[r, :] = dg
        put_heads(p, 1, dot(adapted[r], wv[...]), dg * gate)
        send_heads(2 * p)
        send_heads(2 * p + 1)

    for c in loads[2:]:
        c.wait()
    va_part(0)

    for ib in range(2):
        if ib == 1:
            for k in range(1, 4):
                bias_x(1, k).start()
        bias_y(ib).wait()
        for k in range(1, 4):
            bias_f(ib, k).start()

    qk_part(1)
    va_part(1)
    adT[...] = jnp.transpose(adapted)

    live = mask[...] > 0
    livef = live.astype(f32)
    db_copies = []
    for ib in range(2):
        i, r0 = half_rows(ib)
        rows = pl.ds(r0, R)
        for k in range(1, 4):
            bias_x(ib, k).wait()
            bias_f(ib, k).wait()

        def prep(n, c):
            part = pl.ds(pl.multiple_of(n * 128, 128), 128)
            for b in range(8):
                sl = slice(128 * b, 128 * b + 128)
                tile = G[b // 3, pl.ds(pl.multiple_of(1024 * (b % 3) + r0 + n * 128, 128), 128), :]
                bm[part, sl] = jnp.where(live[:, sl], tile.astype(f32) * LOG2E, masked_score)
                acc[part, sl] = jnp.zeros((128, 128), f32)
            return c

        lax.fori_loop(0, R // 128, prep, 0)

        def sample(s, carry):
            if ib == 0:
                for k in range(1, 16):
                    remote(send.at[s, 0], recv.at[s, 0], q1s.at[s, k], q1r.at[s, k], seq_peer(pos, k)).wait()
                lo64, hi64 = slice(0, 64), slice(64, 128)
                for t, (r, l) in enumerate(((0, lo64), (0, hi64), (48, lo64), (48, hi64))):
                    for b in range(8):
                        sl = slice(128 * b, 128 * b + 128)
                        both = jnp.concatenate([recv[s, 2 * b, r : r + 48, l], recv[s, 2 * b + 1, r : r + 48, l]], axis=1)
                        if t == 1:
                            both = jnp.where(live[:, sl], both.astype(f32), 0.0).astype(bf16)
                        xs[s, 48 * t : 48 * t + 48, sl] = both
            qT = xs[s, 0:48, rows]
            kT = xs[s, 48:96, :]
            vext = jnp.concatenate([xs[s, 96:144, :], jnp.ones((16, T), bf16)], axis=0)
            S = dot(qT, kT, 0, 0) + bm[...]
            m = jnp.max(S, axis=1, keepdims=True)
            e = jnp.exp2(S - m)
            eb = e.astype(bf16)
            av = dot(vext, eb, 1, 1)
            rinv = 1.0 / av[48:49]
            att = av[0:48] * rinv
            da = (xs[s, 144:192, rows].astype(f32) * rinv).astype(bf16)
            delta = jnp.sum(da.astype(f32) * att, axis=0, keepdims=True)
            hi = delta.astype(bf16).astype(f32)
            row = lax.broadcasted_iota(jnp.int32, (16, R), 0)
            corr = jnp.where(row == 0, -hi, jnp.where(row == 1, hi - delta, 0.0)).astype(bf16)
            dS = e * dot(jnp.concatenate([da, corr], axis=0), vext, 0, 0)
            acc[...] += dS
            dSb = dS.astype(bf16)
            dq = (dot(kT, dSb, 1, 1) * (1.0 / math.sqrt(HS))).astype(bf16)
            dk = dot(qT, dSb)
            dv = dot(da, eb)
            att = att.astype(bf16)

            for r in range(8):
                dev = 8 * i + r
                lanes = slice(64 * r, 64 * r + 64)
                send[s, dev, 0:48, :] = jnp.concatenate([att[:, lanes], dq[:, lanes]], axis=1)
            for r in range(8):
                dev = 8 * i + r

                def go():
                    k = lax.rem(dev - me + 16, 16)
                    remote(send.at[s, dev, 0:48], back.at[s, me, 0:48], o1s.at[s, k], o1r.at[s, k], (dev, samp)).start()

                if ib == 0:
                    go()
                else:
                    pl.when(dev != me)(go)
            if ib == 0:
                dkv[s, 0:48, :] = dk
                dkv[s, 48:96, :] = dv
            else:
                back[s, me, 0:48, :] = send[s, me, 0:48, :]
                dk = ((dkv[s, 0:48, :] + dk) * (livef * LN2)).astype(bf16)
                dv = (dkv[s, 48:96, :] + dv).astype(bf16)
                for n in range(16):
                    lanes = slice(64 * n, 64 * n + 64)
                    send[s, n, 48:96, :] = jnp.concatenate([dk[:, lanes], dv[:, lanes]], axis=1)
                for k in range(1, 16):
                    dev = seq_peer(pos, k)
                    remote(send.at[s, dev[0], 48:96], back.at[s, me, 48:96], o2s.at[s, k], o2r.at[s, k], dev).start()
                back[s, me, 48:96, :] = send[s, me, 48:96, :]
            return carry

        lax.fori_loop(0, 4, sample, 0)

        def fin(n, c):
            part = pl.ds(pl.multiple_of(n * 128, 128), 128)
            for b in range(8):
                sl = slice(128 * b, 128 * b + 128)
                DBS[b, pl.ds(pl.multiple_of(r0 + n * 128, 128), 128), :] = (acc[part, sl] * livef[:, sl]).astype(bf16)
            return c

        lax.fori_loop(0, R // 128, fin, 0)
        for k in range(1, 4):
            dev = along(pos, "x", k)
            for y in range(2):
                c = remote(DBS.at[lax.rem(dev[1], 4) + 4 * y, rows], DB.at[k - 1, y, rows],
                           dbs.at[ib, 2 * k + y], dbr.at[ib, 2 * k + y], dev)
                c.start()
                db_copies.append(c)

    def get(t):
        both = [
            jnp.transpose(jnp.concatenate([back[s, h, HS * t : HS * t + HS, :] for h in range(16)], axis=0))
            for s in range(4)
        ]
        return jnp.concatenate([z[0:64] for z in both], axis=0), jnp.concatenate([z[64:128] for z in both], axis=0)

    first = {}
    place = {4: 0, 3: 1, 0: 2, 1: 3, 2: 4}

    def put(m, val):
        at = place[m]
        rows = slice(768 * at, 768 * at + 768)
        for j in range(6):
            G[j, rows, :] = val[:, 128 * j : 128 * j + 128].astype(bf16)
        first[at] = []
        for p in range(3):
            c = remote(G.at[other * 3 + p, rows], R0.at[p, rows], s0s.at[p, at], s0r.at[p, at], core_peer(pos))
            c.start()
            first[at].append(c)

    groups = [(0, 2304, R1a, B1a, R2a, R3a), (2304, 1536, R1b, B1b, R2b, R3b)]
    flying = {}

    def quarter(g, i):
        base, n = groups[g][:2]
        return pl.ds(pl.multiple_of(base + i * (n // 4), 16), n // 4)

    def piece(g, i):
        n = groups[g][1] // 16
        return pl.ds(pl.multiple_of(i * n, 16), n)

    def ring(key, g, p, axis, ss, rs, ref):
        out = []
        for k in range(1, 4):
            src, dst = ref(k)
            c = remote(src, dst, ss.at[g, p, k], rs.at[g, p, k], along(pos, axis, k))
            c.start()
            out.append(c)
        flying[key, g, p] = out

    def land(key, g, p):
        for c in flying[key, g, p]:
            c.wait()

    def scatter1(g):
        base, n, R1 = groups[g][:3]
        for at in range(base // 768, (base + n) // 768):
            for c in first[at]:
                c.wait()
        for p in range(3):
            j = mine[p]
            a1 = AXES[p][0]

            def add(i, carry):
                rows = pl.ds(pl.multiple_of(base + i * 384, 384), 384)
                G[j, rows, :] = (G[j, rows, :].astype(f32) + R0[p, rows, :].astype(f32)).astype(bf16)
                return carry

            lax.fori_loop(0, n // 384, add, 0)
            ring("s1", g, p, a1, s1s, s1r, lambda k: (G.at[j, quarter(g, lax.rem(pos[a1] + k, 4))], R1.at[p, k - 1]))

    def scatter2(g):
        R1, B1, R2 = groups[g][2:5]
        for p in range(3):
            land("s1", g, p)
            a1, a2 = AXES[p][0], AXES[p][1]
            tot = G[mine[p], quarter(g, pos[a1]), :].astype(f32)
            for k in range(3):
                tot = tot + R1[p, k].astype(f32)
            B1[p] = tot.astype(bf16)
            ring("s2", g, p, a2, s2s, s2r, lambda k: (B1.at[p, piece(g, lax.rem(pos[a2] + k, 4))], R2.at[p, k - 1]))

    def exchange(g):
        B1, R2, R3 = groups[g][3:6]
        for p in range(3):
            land("s2", g, p)
            a2, a3 = AXES[p][1], AXES[p][2]
            tot = B1[p, piece(g, pos[a2]), :].astype(f32)
            for k in range(3):
                tot = tot + R2[p, k].astype(f32)
            at = pos[a3]
            R3[p, at] = tot.astype(bf16)
            ring("s3", g, p, a3, s3s, s3r, lambda k: (R3.at[p, at], R3.at[p, at]))

    def gather2(g):
        base, n = groups[g][:2]
        R3 = groups[g][5]
        for p in range(3):
            land("s3", g, p)
            a1, a2 = AXES[p][0], AXES[p][1]
            rows = pl.ds(pl.multiple_of(base + pos[a1] * (n // 4) + pos[a2] * (n // 16), 16), n // 16)
            F[mine[p], rows, :] = (
                R3[p, 0].astype(f32) + R3[p, 1].astype(f32) + R3[p, 2].astype(f32) + R3[p, 3].astype(f32)
            ).astype(bf16)
            ring("g2", g, p, a2, g2s, g2r, lambda k: (F.at[mine[p], rows], F.at[mine[p], rows]))

    cgc = [[], []]

    def to_core(g, p, k, t):
        part = F.at[mine[p], quarter(g, t)]
        c = remote(part, part, gcs.at[g, p, k], gcr.at[g, p, k], core_peer(pos))
        c.start()
        cgc[g].append(c)

    def quarter_part(g, i, half):
        base, n = groups[g][:2]
        return pl.ds(pl.multiple_of(base + i * (n // 4) + half * (n // 8), 16), n // 8)

    def gather1(g):
        for p in range(3):
            land("g2", g, p)
            a1 = AXES[p][0]
            part = F.at[mine[p], quarter(g, pos[a1])]
            out = []
            for n, k in enumerate((1, 3)):
                c = remote(part, part, g1s.at[g, p, n], g1r.at[g, p, n], along(pos, a1, k))
                c.start()
                out.append(c)
            flying["g1", g, p] = out
            to_core(g, p, 0, pos[a1])

    def forward(g):
        for p in range(3):
            a1 = AXES[p][0]
            out = []
            for n, k in enumerate((1, 3)):
                flying["g1", g, p][n].wait()
                t = lax.rem(pos[a1] + 4 - k, 4)
                part = F.at[mine[p], quarter_part(g, t, n)]
                c = remote(part, part, g1s.at[g, p, 2 + n], g1r.at[g, p, 2 + n], along(pos, a1, k))
                c.start()
                out.append(c)
                to_core(g, p, 1 + n, t)
            flying["f1", g, p] = out

    def gather0(g):
        for p in range(3):
            land("f1", g, p)
            to_core(g, p, 3, lax.rem(pos[AXES[p][0]] + 2, 4))

    def home(r, ss, rs):
        for s in range(4):
            for k in range(1, 16):
                part = slice(r, r + 48)
                remote(send.at[s, 0, part], back.at[s, 0, part], ss.at[s, k], rs.at[s, k], seq_peer(pos, k)).wait()

    home(0, o1s, o1r)
    cot = dout[...].astype(f32)
    gs = sig[...]
    att, dq = get(0)
    att = att.astype(f32)
    gated = (gs * att).astype(bf16)
    put(4, dot(gated, dproj[...], 0, 0))
    dgl = (dgated[...] * att * gs * (1.0 - gs)).astype(bf16)
    put(3, dot(adT[...], dgl))
    put(0, dot(adT[...], dq))
    scatter1(0)
    home(48, o2s, o2r)
    dk, dv = get(1)
    dxs = [dq, dk, dv]
    put(1, dot(adT[...], dk))
    put(2, dot(adT[...], dv))
    scatter1(1)

    normed, inv = norm_rows(tok[...].astype(f32))
    dog[...] = (cot * dot(gated, wo[...])).astype(bf16)
    d_ad = dot(dgl, wg[...], 1, 1)
    for m, w in enumerate((wq, wk, wv)):
        d_ad = d_ad + dot(dxs[m], w[...], 1, 1)
    dshift[...] = d_ad.astype(bf16)
    dscale[...] = (d_ad * normed).astype(bf16)
    dn = d_ad * scale[...].astype(f32)
    m1 = jnp.mean(dn, axis=-1, keepdims=True)
    m2 = jnp.mean(dn * normed, axis=-1, keepdims=True)
    dtok[...] = (cot + inv * (dn - m1 - normed * m2)).astype(bf16)

    scatter2(0)
    scatter2(1)

    for c in db_copies:
        c.wait()

    def sum_bias(i, carry):
        rows = pl.ds(pl.multiple_of(i * 128, 128), 128)
        for y in range(2):
            b = pos["x"] + 4 * y
            tot = DBS[b, rows, :].astype(f32)
            for k in range(3):
                tot = tot + DB[k, y, rows, :].astype(f32)
            SB[y, rows, :] = tot.astype(bf16)
        return carry

    lax.fori_loop(0, 8, sum_bias, 0)
    yhi = samp // 4
    hand = remote(SB.at[1 - yhi], DY, dys.at[0], dyr.at[0], samp_peer(pos, 4))
    hand.start()

    exchange(0)
    exchange(1)
    gather2(0)
    gather2(1)
    gather1(0)
    gather1(1)

    hand.wait()

    def sum_half(i, carry):
        rows = pl.ds(pl.multiple_of(i * 128, 128), 128)
        SB[yhi, rows, :] = (SB[yhi, rows, :].astype(f32) + DY[rows, :].astype(f32)).astype(bf16)
        return carry

    lax.fori_loop(0, 8, sum_half, 0)
    pr = []
    for k in range(1, 16):
        dev = seq_peer(pos, k)
        rows = pl.ds(pl.multiple_of(dev[0] * 64, 64), 64)
        c = remote(SB.at[yhi, rows], RP.at[me], prs.at[k - 1], prr.at[k - 1], dev)
        c.start()
        pr.append(c)
    RP[me] = SB[yhi, pl.ds(pl.multiple_of(me * 64, 64), 64), :]

    forward(0)
    forward(1)
    out_copies = []

    def leave(g, first_slab):
        base, n = groups[g][:2]
        for p in range(3):
            part = (first_slab + p, slice(base, base + n))
            c = pltpu.make_async_copy(F.at[part], F_out.at[part], fs.at[len(out_copies)])
            c.start()
            out_copies.append(c)

    gather0(0)
    leave(0, core * 3)
    gather0(1)
    leave(1, core * 3)
    for g in range(2):
        for c in cgc[g]:
            c.wait()
        leave(g, other * 3)
    for c in pr + out_copies:
        c.wait()


def widen_kernel(F, RP, *refs):
    acts, outs = refs[:4], refs[4:]
    for i in range(4):
        outs[i][...] = acts[i][...]
    outs[4][...] = RP[...].astype(f32)
    for m, at in ((0, 2), (1, 3), (2, 4), (3, 1), (4, 0)):
        for j in range(6):
            outs[5 + m][:, 128 * j : 128 * j + 128] = F[j, at].astype(f32)


def sds(shape, dtype):
    return jax.ShapeDtypeStruct(shape, dtype)


def on_device(tokens, ada_scale, ada_shift, out_gate, d_out, pair_bias, key_mask,
              w_query, w_key, w_value, w_gate, w_output):
    dma = lambda *shape: pltpu.SemaphoreType.DMA(shape)
    rows = lambda a: a.reshape(256, 768)
    tok, scale, shift, og, cot = map(rows, (tokens, ada_scale, ada_shift, out_gate, d_out))
    heads = V((4, 16, 96, 128), bf16)
    dtok, dscale, dshift, dog, F, RP = pl.pallas_call(
        block_kernel,
        out_shape=(sds((256, 768), bf16),) * 4 + (sds((6, 3840, 128), bf16), sds((16, 64, 128), bf16)),
        in_specs=[spec()] * 7 + [pl.BlockSpec(memory_space=pl.ANY)] * 5,
        out_specs=[spec()] * 4 + [pl.BlockSpec(memory_space=pl.ANY), spec()],
        scratch_shapes=[V((6, 3840, 128), bf16), V((5, 768, 768), bf16), heads, heads, heads, V((1024, 128), bf16), V((512, 1024), f32), V((512, 1024), f32),
                        V((4, 192, 1024), bf16), V((4, 96, 1024), f32), V((256, 768), f32), V((256, 768), f32), V((768, 256), bf16), V((256, 768), bf16),
                        V((6, 3840, 128), bf16), V((3, 3840, 128), bf16)]
        + [V(shape, bf16) for q in (576, 384)
           for shape in ((3, 3, q, 128), (3, q, 128), (3, 3, q // 4, 128), (3, 4, q // 4, 128))]
        + [V((8, 1024, 128), bf16), V((3, 2, 1024, 128), bf16), V((2, 1024, 128), bf16), V((1024, 128), bf16)]
        + [dma(16)] * 2 + [dma(4, 4)] * 2 + [dma(4)] * 2 + [dma(4, 4)] * 2 + [dma(4, 16)] * 6
        + [dma(3, 5)] * 2 + [dma(2, 3, 4)] * 12 + [dma(2, 8)] * 2 + [dma(1)] * 2 + [dma(15)] * 2 + [dma(5), dma(12)],
        compiler_params=pltpu.CompilerParams(vmem_limit_bytes=VMEM_LIMIT, collective_id=2, has_side_effects=True),
        cost_estimate=pl.CostEstimate(flops=16 * 10**9, bytes_accessed=20 << 20, transcendentals=5 << 20),
    )(tok, scale, shift, og, cot, pair_bias, key_mask.reshape(1, 1024), w_query, w_key, w_value, w_gate, w_output)
    act = pl.BlockSpec((32, 768), lambda i: (i, 0))
    tile = pl.BlockSpec((2, 64, 128), lambda i: (i, 0, 0))
    outs = pl.pallas_call(
        widen_kernel,
        grid=(8,),
        out_shape=(sds((256, 768), bf16),) * 4 + (sds((16, 64, 128), f32),) + (sds((768, 768), f32),) * 5,
        in_specs=[pl.BlockSpec((6, 5, 96, 128), lambda i: (0, 0, i, 0)), tile] + [act] * 4,
        out_specs=[act] * 4 + [tile] + [pl.BlockSpec((96, 768), lambda i: (i, 0))] * 5,
    )(F.reshape(6, 5, 768, 128), RP, dtok, dscale, dshift, dog)
    shaped = lambda a: a.reshape(4, 64, 768)
    return tuple(map(shaped, outs[:4])) + tuple(outs[4:])


def solution(mesh):
    act = P("samp", "seq", None)
    tile = P(None, "seq", "samp")
    return jax.shard_map(
        on_device,
        mesh=mesh,
        in_specs=(act,) * 5 + (tile,) + (P(),) * 6,
        out_specs=(act,) * 4 + (tile,) + (P(),) * 5,
        check_vma=False,
    )
```
